256 devices in a mesh: tiles: 64 (over x, z, core), sub: 4 (over y).
Axes of the slice: x: 4, y: 4, z: 8, core: 2. Of those that a mesh axis runs over, the one named last changes fastest.
Arguments:
- floe_area: float32 [5, 16, 32, 32768], P(None, None, 'sub', 'tiles'), may hold values from 0 to 1
- courant: float32 [2, 32, 32768], P(None, 'sub', 'tiles'), may hold values from -0.45 to 0.45
- spectra: bfloat16 [64, 4, 512, 1296], P('tiles', 'sub'), may hold values from 0.0049743652 to 0.5
- send_rows: int32 [64, 4, 64, 4, 4], P('tiles', 'sub'), may hold values from 0 to 511
- src_slot: int32 [4, 32, 32768], P(None, 'sub', 'tiles'), may hold values from 0 to 1023
- src_weight: float32 [4, 32, 32768], P(None, 'sub', 'tiles'), may hold values from 0.1 to 0.5
- thickness: float32 [32, 32768], P('sub', 'tiles'), may hold values from 0.3 to 3
- edge_angle: float32 [32, 32768], P('sub', 'tiles'), may hold values from -3.140625 to 3.140625
- decay_rate: float32 [36], replicated, may hold values from 0.05 to 0.5
- strain_table: bfloat16 [16, 1296], replicated, may hold values from 0.0009994507 to 1
- ice_mask: int32 [32, 32768], P('sub', 'tiles'), may hold values 0 or 1
- break_bin: int32 [32, 32768], P('sub', 'tiles'), may hold values from 1 to 15
Outputs:
- fractured: float32 [5, 16, 32, 32768], P(None, None, 'sub', 'tiles')
The draws below stay inside these ranges and needn't reach their ends.
Inputs may be any that keep to these rules, and one draw needn't show every extreme that they name: `send_rows`: wave cells numbered within the sending device; every device sends exactly 4 spectra to every device. `src_slot`: slots numbered in the order of the sending device's tiles index, then its sub index, then the slot.
All inputs are finite; a program needn't handle non-finite values. No bound on the sum of `ice_mask` on one device may be relied on, other than what follows from the above.
Results may differ from the reference program's by a relative error of at most 0.0003.
Values may be sent and summed in bfloat16 or wider, within the bound.
A program may use at most 64 MiB of HBM per device.

```python
import math
import jax
import jax.numpy as jnp
from jax import lax

NCAT = 5
NFSD = 16
NFREQ = 36
NDIR = 36
NBIN = 1296
CR = 8
CC = 512
WC = 512
CAP = 4
KSRC = 4
NSUB = 3
ROWS = 32
COLS = 32768
N_TILES = 64
N_SUB = 4


def set_ends(drawn, stream_key, smallest, largest):
    longest = drawn.shape.index(max(drawn.shape))
    spots = []
    for shift in (0, 1):
        where = [jax.random.randint(jax.random.fold_in(stream_key, axis), (), 0, length) for axis, length in enumerate(drawn.shape)]
        where[longest] = (where[longest] + shift) % drawn.shape[longest]
        spots.append(tuple(where))
    return drawn.at[spots[0]].set(smallest).at[spots[1]].set(largest)


def block_scale(stream_key, extent, shards, least, high):
    loudness = 1.0
    for position, shards_of in shards:
        steps = jax.random.uniform(jax.random.fold_in(jax.random.fold_in(stream_key, 6), position), (shards_of,), jnp.float32, least / len(shards), high / len(shards))
        loudness = loudness * jnp.repeat(jnp.exp(steps), extent[position] // shards_of).reshape((-1,) + (1,) * (len(extent) - 1 - position))
    return loudness


def setup_inputs(seed: int = 0) -> dict:
    key_list = jax.random.split(jax.random.key(seed), 13)
    return {
        "floe_area": jnp.clip(1.0 * jax.random.uniform(key_list[0], (NCAT, NFSD, ROWS, COLS), jnp.float32) ** block_scale(key_list[0], (NCAT, NFSD, ROWS, COLS), ((2, 4), (3, 64)), -0.2, 0.2), 0.0, 1.0),
        "courant": jnp.clip(jax.random.uniform(key_list[1], (2, ROWS, COLS), jnp.float32, -0.45, 0.45) * block_scale(key_list[1], (2, ROWS, COLS), ((1, 4), (2, 64)), -0.4, 0.0), -0.45, 0.45),
        "spectra": jnp.clip(jnp.exp(math.log(0.5) - 4.61031033 * jax.random.uniform(key_list[2], (N_TILES, N_SUB, WC, NBIN), jnp.float32) ** block_scale(key_list[2], (N_TILES, N_SUB, WC, NBIN), ((0, 64), (1, 4)), -0.2, 0.2)), 0.0049743652, 0.5).astype(jnp.bfloat16),
        "send_rows": set_ends(jax.random.randint(key_list[3], (N_TILES, N_SUB, N_TILES, N_SUB, CAP), 0, WC), jax.random.fold_in(key_list[3], 1), 0, WC - 1).astype(jnp.int32),
        "src_slot": set_ends(jax.random.randint(key_list[4], (KSRC, ROWS, COLS), 0, N_TILES * N_SUB * CAP), jax.random.fold_in(key_list[4], 1), 0, (N_TILES * N_SUB * CAP) - 1).astype(jnp.int32),
        "src_weight": jnp.clip(0.1 + 0.4 * jax.random.uniform(key_list[5], (KSRC, ROWS, COLS), jnp.float32) ** block_scale(key_list[5], (KSRC, ROWS, COLS), ((1, 4), (2, 64)), -0.2, 0.2), 0.1, 0.5),
        "thickness": jnp.clip(0.3 + 2.7 * jax.random.uniform(key_list[6], (ROWS, COLS), jnp.float32) ** block_scale(key_list[6], (ROWS, COLS), ((0, 4), (1, 64)), -0.2, 0.2), 0.3, 3.0),
        "edge_angle": jnp.clip(jax.random.uniform(key_list[7], (ROWS, COLS), jnp.float32, -3.140625, 3.140625), -3.140625, 3.140625),
        "decay_rate": jnp.clip(jnp.exp(jax.random.uniform(key_list[8], (NFREQ,), jnp.float32, math.log(0.05), math.log(0.5))), 0.05, 0.5),
        "strain_table": jnp.clip(jnp.exp(jax.random.uniform(key_list[9], (NFSD, NBIN), jnp.float32, math.log(0.0009994507), math.log(1.0))), 0.0009994507, 1.0).astype(jnp.bfloat16),
        "ice_mask": set_ends((jax.random.randint(key_list[10], (ROWS, COLS), 0, 4) < 3).astype(jnp.int32), jax.random.fold_in(key_list[10], 1), 0, 1),
        "break_bin": set_ends(jax.random.randint(key_list[11], (ROWS, COLS), 1, NFSD), jax.random.fold_in(key_list[11], 1), 1, NFSD - 1).astype(jnp.int32),
    }


def damping(decay_rate, thick_cells, edge_cells, dir_count):
    angles = 2.0 * math.pi * jnp.arange(dir_count, dtype=jnp.int32).astype(jnp.float32) / dir_count - math.pi
    cosine = jnp.cos(angles[None, :] - edge_cells[:, None])
    path_length = 1.0 / (0.25 + 0.75 * cosine * cosine)
    exponent = decay_rate[None, :, None] * thick_cells[:, None, None] * path_length[:, None, :]
    return jnp.exp(-exponent).reshape(thick_cells.shape[0], -1)


def fracture(moved, hist, ice_cells, break_cells, bin_count):
    total_hist = jnp.sum(hist, axis=0)
    hist_share = hist / total_hist
    strength = ice_cells.astype(jnp.float32) * total_hist / (total_hist + 0.005 * hist.shape[0] * bin_count)
    shorter = jnp.cumsum(hist_share, axis=0) - hist_share
    size_bins = jnp.arange(hist.shape[0], dtype=jnp.int32)[:, None]
    allowed = (size_bins >= break_cells[None, :]).astype(jnp.float32)
    breakable = moved * allowed[None]
    above_sum = jnp.sum(breakable, axis=1, keepdims=True) - jnp.cumsum(breakable, axis=1)
    return moved - breakable * (strength * shorter)[None] + above_sum * (strength * hist_share)[None]


def advance(values, courant):
    east_part = jnp.maximum(courant[0], 0.0)
    west_part = jnp.maximum(-courant[0], 0.0)
    north_part = jnp.maximum(courant[1], 0.0)
    south_part = jnp.maximum(-courant[1], 0.0)
    keep_part = 1.0 - east_part - west_part - north_part - south_part
    result = values * keep_part
    result = result + jnp.roll(values * east_part, 1, axis=2)
    result = result + jnp.roll(values * west_part, -1, axis=2)
    result = result + jnp.pad(values * north_part, ((0, 0), (1, 0), (0, 0)))[:, :-1]
    result = result + jnp.pad(values * south_part, ((0, 0), (0, 1), (0, 0)))[:, 1:]
    return result


def reference(floe_area, courant, spectra, send_rows, src_slot, src_weight, thickness, edge_angle, decay_rate, strain_table, ice_mask, break_bin):
    moved = floe_area.reshape(NCAT * NFSD, ROWS, COLS)
    for substep in range(NSUB):
        moved = advance(moved, courant)
    moved = moved.reshape(NCAT, NFSD, ROWS, COLS)
    flat_waves = spectra.reshape(N_TILES * N_SUB * WC, NBIN)
    col_tile = jnp.arange(COLS, dtype=jnp.int32) // CC

    def one_row(pieces):
        row_number, slot_row, weight_row, thick_row, edge_row, ice_row, break_row, moved_row = pieces
        row_sub = row_number // CR
        spectrum = jnp.zeros((COLS, NBIN), jnp.float32)
        for source in range(KSRC):
            slot_now = slot_row[source]
            sender_tile = slot_now // (N_SUB * CAP)
            sender_sub = (slot_now // CAP) % N_SUB
            slot_place = slot_now % CAP
            wave_cell = send_rows[sender_tile, sender_sub, col_tile, row_sub, slot_place]
            picked = flat_waves[(sender_tile * N_SUB + sender_sub) * WC + wave_cell].astype(jnp.float32)
            if source == 0:
                spectrum = weight_row[source][:, None] * picked
            else:
                spectrum = spectrum + weight_row[source][:, None] * picked
        attenuated = (spectrum * damping(decay_rate, thick_row, edge_row, NDIR)).astype(jnp.bfloat16)
        hist = lax.dot_general(strain_table, attenuated, (((1,), (1,)), ((), ())), preferred_element_type=jnp.float32)
        return fracture(moved_row, hist, ice_row, break_row, NBIN)

    row_results = lax.map(one_row, (jnp.arange(ROWS, dtype=jnp.int32), jnp.transpose(src_slot, (1, 0, 2)), jnp.transpose(src_weight, (1, 0, 2)), thickness, edge_angle, ice_mask, break_bin, jnp.transpose(moved, (2, 0, 1, 3))))
    return jnp.transpose(row_results, (1, 2, 0, 3))
```

```python
import functools
import math

import jax
import jax.numpy as jnp
from jax import lax
from jax.experimental import pallas as pl
from jax.experimental.pallas import tpu as pltpu
from jax.sharding import PartitionSpec as P

MESH = pl.DeviceIdType.MESH
F32 = jnp.float32
BF16 = jnp.bfloat16
NDIR = 36
NBIN = 1296
NSUB = 3
N_DEV = 256
SPLIT = 1024
TAIL = 384


def coords():
    t, s = lax.axis_index("tiles"), lax.axis_index("sub")
    return t // 16, lax.rem(t, 16), s


def zc_peer(i, x, zc, s):
    c = lax.rem(lax.rem(zc, 2) + i % 2, 2)
    z = lax.rem(zc // 2 + i // 2, 8)
    return (x * 16 + z * 2 + c, s)


def xy_peer(i, x, zc, s):
    return (lax.rem(x + i // 4, 4) * 16 + zc, lax.rem(s + i % 4, 4))


def exchange_kernel(xa, xb, ra, rb, send_sem, recv_a, recv_b, own_sem, group_sem):
    x, zc, s = coords()
    me = (x * 16 + zc) * 4 + s
    barrier = pltpu.get_barrier_semaphore()
    for i in range(1, 16):
        pl.semaphore_signal(barrier, inc=1, device_id=zc_peer(i, x, zc, s), device_id_type=MESH)
        pl.semaphore_signal(barrier, inc=1, device_id=xy_peer(i, x, zc, s), device_id_type=MESH)
    pl.semaphore_wait(barrier, 30)
    for i in range(1, 16):
        pl.semaphore_signal(group_sem, inc=1, device_id=xy_peer(i, x, zc, s), device_id_type=MESH)
    pl.semaphore_wait(group_sem, 15)
    own_a = pltpu.make_async_copy(xa.at[me], ra.at[me], own_sem.at[0])
    own_b = pltpu.make_async_copy(xb.at[me], rb.at[me], own_sem.at[1])
    own_a.start()
    own_b.start()

    def sender(src, dst, sem, slot):
        def one(i, carry):
            c = lax.rem(lax.rem(zc, 2) + lax.rem(i, 2), 2)
            z = lax.rem(zc // 2 + lax.rem(i // 2, 8), 8)
            tile = lax.rem(x + i // 64, 4) * 16 + z * 2 + c
            sub = lax.rem(s + lax.rem(i // 16, 4), 4)
            pltpu.make_async_remote_copy(
                src_ref=src.at[tile * 4 + sub],
                dst_ref=dst.at[me],
                send_sem=send_sem.at[slot],
                recv_sem=sem,
                device_id=(tile, sub),
                device_id_type=MESH,
            ).start()
            return carry

        lax.fori_loop(1, N_DEV, one, 0)

    sender(xa, ra, recv_a, 0)
    sender(xb, rb, recv_b, 1)
    own_a.wait()
    own_b.wait()
    rest = pl.ds(0, N_DEV - 1)
    pltpu.make_async_copy(xa.at[rest], ra.at[rest], recv_a).wait()
    pltpu.make_async_copy(xb.at[rest], rb.at[rest], recv_b).wait()
    pltpu.make_async_copy(xa.at[rest], ra.at[rest], send_sem.at[0]).wait()
    pltpu.make_async_copy(xb.at[rest], rb.at[rest], send_sem.at[1]).wait()


def exchange(xa, xb):
    vmem = pl.BlockSpec(memory_space=pltpu.VMEM)
    return pl.pallas_call(
        exchange_kernel,
        out_shape=[jax.ShapeDtypeStruct(v.shape, v.dtype) for v in (xa, xb)],
        in_specs=[vmem] * 2,
        out_specs=[vmem] * 2,
        scratch_shapes=[
            pltpu.SemaphoreType.DMA((2,)),
            pltpu.SemaphoreType.DMA(()),
            pltpu.SemaphoreType.DMA(()),
            pltpu.SemaphoreType.DMA((2,)),
            pltpu.SemaphoreType.REGULAR,
        ],
        compiler_params=pltpu.CompilerParams(
            collective_id=0, has_side_effects=True, vmem_limit_bytes=50 << 20
        ),
    )(xa, xb)


def transpose_in(src, table, first, width):
    for lane in range(0, width, 128):
        size = min(128, width - lane)
        block = src[:, :, lane : lane + 128].reshape(N_DEV * 4, 128)
        turned = block.T
        table[first + lane : first + lane + size, :] = turned[:size]


def build_mixing(r, slot, weight, mixing):
    rows = lax.broadcasted_iota(jnp.int32, (N_DEV * 4, 512), 0).astype(jnp.int16)
    total = jnp.zeros((N_DEV * 4, 512), BF16)
    for k in range(4):
        slots = slot[k, pl.ds(r, 1), :].astype(jnp.int16)
        weights = weight[k, pl.ds(r, 1), :].astype(BF16)
        total = total + jnp.where(rows == slots, weights, jnp.zeros((), BF16))
    mixing[...] = total


def wide(column, lanes=4):
    return jnp.concatenate([column] * lanes, axis=1)


def fill_decay(decay, decay_table):
    row = lax.broadcasted_iota(jnp.int32, (72, 128), 0)
    for g in range(18):
        decay_table[g * 72 : g * 72 + 72, :] = jnp.where(row < 36, decay[2 * g], decay[2 * g + 1])


def path_table(r, thick, edge, trig):
    edge_row = edge[pl.ds(r, 1), :]
    cos_row, sin_row = jnp.cos(edge_row), jnp.sin(edge_row)
    cosine = wide(trig[0]) * cos_row + wide(trig[1]) * sin_row
    return (-math.log2(math.e) * thick[pl.ds(r, 1), :]) / (0.25 + 0.75 * cosine * cosine)


def attenuate(first, size, table, mixing, decay_table, path, att):
    step = 144
    for start in range(first, first + size, step):
        spectrum = jnp.dot(table[start : start + step, :], mixing[...], preferred_element_type=F32)
        decay_rows = wide(decay_table[start : start + step, :])
        damping = jnp.exp2(decay_rows * jnp.concatenate([path] * (step // 72), axis=0))
        att[start : start + step, :] = (spectrum * damping).astype(BF16)


def fracture(hist, weight, ice, brk, moved, out):
    total_w = weight[0] + weight[1] + weight[2] + weight[3]
    used_w = sum(weight[k].astype(BF16).astype(F32) for k in range(4))
    fix = total_w / used_w
    rows = [hist[j] * fix for j in range(16)]
    total = functools.reduce(jnp.add, rows)
    strength = ice[...].astype(F32) * total / (total + 0.005 * 16 * NBIN)
    scale = strength / total
    share = [v * scale for v in rows]
    shorter, run = [], jnp.zeros_like(total)
    for j in range(16):
        shorter.append(run)
        run = run + share[j]
    brk_rows = brk[...]
    for n in range(5):
        above = jnp.zeros_like(total)
        for k in range(15, -1, -1):
            value = moved[n, k]
            breakable = jnp.where(brk_rows <= k, value, 0.0)
            out[n, k] = value - breakable * shorter[k] + above * share[k]
            above = above + breakable


def remap_kernel(
    decay, ra, rb, slot, weight, thick, edge, strain, ice, brk, moved, trig, out,
    table, mixing, decay_table, att, hist
):
    fill_decay(decay, decay_table)
    transpose_in(ra, table, 0, SPLIT)
    transpose_in(rb, table, SPLIT, NBIN - SPLIT)

    def one_row(r, carry):
        build_mixing(r, slot, weight, mixing)
        path = path_table(r, thick, edge, trig)
        attenuate(0, NBIN, table, mixing, decay_table, path, att)
        row_hist = jnp.dot(strain[...], att[...], preferred_element_type=F32)
        hist[:, pl.ds(r, 1), :] = row_hist[:, None, :]
        return carry

    lax.fori_loop(0, 8, one_row, 0)
    fracture(hist, weight, ice, brk, moved, out)


def remap(ra, rb, slot, weight, thick, edge, decay, strain, ice, brk, moved):
    angles = 2.0 * math.pi * (jnp.arange(72) % NDIR).astype(F32) / NDIR - math.pi
    trig = jnp.broadcast_to(jnp.stack([jnp.cos(angles), jnp.sin(angles)])[:, :, None], (2, 72, 128))
    vmem = pl.BlockSpec(memory_space=pltpu.VMEM)
    return pl.pallas_call(
        remap_kernel,
        out_shape=jax.ShapeDtypeStruct(moved.shape, F32),
        in_specs=[pl.BlockSpec(memory_space=pltpu.SMEM)] + [vmem] * 11,
        out_specs=vmem,
        scratch_shapes=[
            pltpu.VMEM((NBIN, N_DEV * 4), BF16),
            pltpu.VMEM((N_DEV * 4, 512), BF16),
            pltpu.VMEM((NBIN, 128), F32),
            pltpu.VMEM((NBIN, 512), BF16),
            pltpu.VMEM((16, 8, 512), F32),
        ],
        compiler_params=pltpu.CompilerParams(vmem_limit_bytes=50 << 20),
    )(decay, ra, rb, slot, weight, thick, edge, strain, ice, brk, moved, trig)


def transport_kernel(ext, out):
    east = jnp.maximum(ext[80], 0.0)
    west = jnp.maximum(-ext[80], 0.0)
    north = jnp.maximum(ext[81], 0.0)
    south = jnp.maximum(-ext[81], 0.0)
    keep = 1.0 - east - west - north - south

    def one(layer, carry):
        v = ext[layer]
        for _ in range(NSUB):
            v = (
                v * keep
                + pltpu.roll(v * east, 1, 1)
                + pltpu.roll(v * west, 639, 1)
                + pltpu.roll(v * north, 1, 0)
                + pltpu.roll(v * south, 15, 0)
            )
        out[layer] = v[0:8, 0:512]
        return carry

    lax.fori_loop(0, 80, one, 0)


def transport(floe, courant):
    joined = jnp.concatenate([floe.reshape(80, 8, 512), courant], axis=0)
    n_sub, n_tiles = lax.axis_size("sub"), lax.axis_size("tiles")
    below = lax.ppermute(joined[:, 0:3], "sub", [(i + 1, i) for i in range(n_sub - 1)])
    above = lax.ppermute(joined[:, 5:8], "sub", [(i, i + 1) for i in range(n_sub - 1)])
    rows = jnp.concatenate([joined, below, jnp.zeros((82, 2, 512), F32), above], axis=1)
    right = lax.ppermute(rows[:, :, 0:3], "tiles", [((i + 1) % n_tiles, i) for i in range(n_tiles)])
    left = lax.ppermute(rows[:, :, 509:], "tiles", [(i, (i + 1) % n_tiles) for i in range(n_tiles)])
    ext = jnp.concatenate([rows, right, jnp.zeros((82, 16, 122), F32), left], axis=2)
    return pl.pallas_call(
        transport_kernel,
        out_shape=jax.ShapeDtypeStruct((80, 8, 512), F32),
        in_specs=[pl.BlockSpec(memory_space=pltpu.VMEM)],
        out_specs=pl.BlockSpec(memory_space=pltpu.VMEM),
        compiler_params=pltpu.CompilerParams(vmem_limit_bytes=50 << 20),
    )(ext)


def shards(
    floe_area, courant, spectra, send_rows, src_slot, src_weight, thickness, edge_angle,
    decay_rate, strain_table, ice_mask, break_bin
):
    moved = transport(floe_area, courant).reshape(floe_area.shape)
    picks = send_rows.reshape(N_DEV * 4)
    choose = (picks[:, None] == jnp.arange(512, dtype=jnp.int32)[None, :]).astype(BF16)
    outgoing = jnp.dot(choose, spectra[0, 0], preferred_element_type=F32).astype(BF16)
    outgoing = outgoing.reshape(N_DEV, 4, NBIN)
    tail = jnp.pad(outgoing[:, :, SPLIT:], ((0, 0), (0, 0), (0, SPLIT + TAIL - NBIN)))
    ra, rb = exchange(outgoing[:, :, :SPLIT], tail)
    return remap(
        ra, rb, src_slot, src_weight, thickness, edge_angle, decay_rate, strain_table,
        ice_mask, break_bin, moved
    )


def solution(mesh):
    in_specs = (
        P(None, None, "sub", "tiles"),
        P(None, "sub", "tiles"),
        P("tiles", "sub", None, None),
        P("tiles", "sub", None, None, None),
        P(None, "sub", "tiles"),
        P(None, "sub", "tiles"),
        P("sub", "tiles"),
        P("sub", "tiles"),
        P(),
        P(),
        P("sub", "tiles"),
        P("sub", "tiles"),
    )
    out_specs = P(None, None, "sub", "tiles")
    return jax.shard_map(shards, mesh=mesh, in_specs=in_specs, out_specs=out_specs, check_vma=False)
```

```python
import functools
import math

import jax
import jax.numpy as jnp
import numpy as np
from jax import lax
from jax.experimental import pallas as pl
from jax.experimental.pallas import tpu as pltpu
from jax.sharding import PartitionSpec as P

MESH = pl.DeviceIdType.MESH
F32 = jnp.float32
BF16 = jnp.bfloat16
NDIR = 36
NBIN = 1296
NSUB = 3
N_DEV = 256
SPLIT = 1024
TAIL = 384
COLUMN_ROWS = 768


def coords():
    t, s = lax.axis_index("tiles"), lax.axis_index("sub")
    return t // 16, lax.rem(t, 16), s


def zc_peer(i, x, zc, s):
    c = lax.rem(lax.rem(zc, 2) + i % 2, 2)
    z = lax.rem(zc // 2 + i // 2, 8)
    return (x * 16 + z * 2 + c, s)


def xy_peer(i, x, zc, s):
    return (lax.rem(x + i // 4, 4) * 16 + zc, lax.rem(s + i % 4, 4))


def tile_of(x, zc, dx, dz, dc):
    core = lax.rem(lax.rem(zc, 2) + dc, 2)
    return lax.rem(x + dx, 4) * 16 + lax.rem(zc // 2 + dz, 8) * 2 + core


def send_all(src, dst, send_sem, recv_sem):
    x, zc, s = coords()
    me = (x * 16 + zc) * 4 + s

    def one(i, carry):
        tile = tile_of(x, zc, i // 64, lax.rem(i // 2, 8), lax.rem(i, 2))
        sub = lax.rem(s + lax.rem(i // 16, 4), 4)
        pltpu.make_async_remote_copy(
            src_ref=src.at[tile * 4 + sub],
            dst_ref=dst.at[me],
            send_sem=send_sem,
            recv_sem=recv_sem,
            device_id=(tile, sub),
            device_id_type=MESH,
        ).start()
        return carry

    lax.fori_loop(1, N_DEV, one, 0)


def gather_rows(picks, spectra, xa, xb):
    pick = picks[...].astype(F32).reshape(N_DEV, 1, 4)
    pick = jnp.broadcast_to(pick, (N_DEV, 4, 4)).reshape(N_DEV * 4, 4)
    row = lax.broadcasted_iota(jnp.int32, (N_DEV * 4, 4), 0)
    lane = lax.broadcasted_iota(jnp.int32, (N_DEV * 4, 4), 1)
    column = jnp.sum(jnp.where(lane == lax.rem(row, 4), pick, 0.0), axis=1, keepdims=True)
    column = column.astype(jnp.int32)
    cell = lax.broadcasted_iota(jnp.int32, (256, 512), 1)
    for b in range(4):
        choose = jnp.where(cell == column[b * 256 : b * 256 + 256], 1.0, 0.0).astype(BF16)
        rows = jnp.dot(choose, spectra[...], preferred_element_type=F32).astype(BF16)
        devices = pl.ds(b * 64, 64)
        xa[devices] = rows[:, :SPLIT].reshape(64, 4, SPLIT)
        rest = jnp.concatenate(
            [rows[:, SPLIT:], jnp.zeros((256, SPLIT + TAIL - NBIN), BF16)], axis=1
        )
        xb[devices] = rest.reshape(64, 4, TAIL)


def pack_halo(floe, courant, row_send, col_send):
    for n in range(5):
        row_send[0, n * 16 : n * 16 + 16] = floe[n, :, 0:4, :]
        row_send[1, n * 16 : n * 16 + 16] = floe[n, :, 4:8, :]
    row_send[0, 80:82] = courant[:, 0:4, :]
    row_send[1, 80:82] = courant[:, 4:8, :]
    filler = jnp.zeros((COLUMN_ROWS - 656, 128), F32)
    for side, lanes in ((0, slice(0, 128)), (1, slice(384, 512))):
        strip = jnp.concatenate(
            [floe[:, :, :, lanes].reshape(640, 128), courant[:, :, lanes].reshape(16, 128), filler]
        )
        turned = strip.T
        col_send[side] = turned[0:8] if side == 0 else turned[120:128]


def halo_copies(row_send, row_recv, col_send, col_recv, send_sem, recv_sem):
    t, s = lax.axis_index("tiles"), lax.axis_index("sub")
    n_tiles = lax.axis_size("tiles")
    copies = []

    def add(src, dst, device):
        k = len(copies)
        copies.append(
            pltpu.make_async_remote_copy(
                src_ref=src,
                dst_ref=dst,
                send_sem=send_sem.at[k],
                recv_sem=recv_sem.at[k],
                device_id=device,
                device_id_type=MESH,
            )
        )

    for side, step in ((0, n_tiles - 1), (1, 1)):
        for group, shift in ((0, 0), (1, 3), (2, 1)):
            device = (lax.rem(t + step, n_tiles), lax.rem(s + shift, 4))
            add(col_send.at[side], col_recv.at[side, group], device)
    add(row_send.at[0], row_recv.at[0], (t, lax.rem(s + 3, 4)))
    add(row_send.at[1], row_recv.at[1], (t, lax.rem(s + 1, 4)))
    return copies


def unpack_columns(col_recv, side):
    for group in range(3):
        side[group] = jnp.concatenate(
            [col_recv[0, group], jnp.zeros((112, COLUMN_ROWS), F32), col_recv[1, group]], axis=0
        ).T


def transport(floe, courant, row_recv, side, out):
    s = lax.axis_index("sub")
    row = lax.broadcasted_iota(jnp.int32, (8, 128), 0)

    def frame(own, layer):
        start = layer * 8 if isinstance(layer, int) else pl.multiple_of(layer * 8, 8)
        here = pl.ds(start, 8)
        corner = jnp.where(row < 4, side[1, here], side[2, here])
        top = jnp.concatenate([own, side[0, here]], axis=1)
        halo = jnp.concatenate([row_recv[0, layer], row_recv[1, layer]], axis=0)
        return top, jnp.concatenate([halo, corner], axis=1)

    wide_row = lax.broadcasted_iota(jnp.int32, (8, 640), 0)
    after, before = jnp.where(s < 3, 1.0, 0.0), jnp.where(s > 0, 1.0, 0.0)
    inside = jnp.where(wide_row < 4, after, before)
    parts = []
    for k in range(2):
        top, halo = frame(courant[k], 80 + k)
        parts.append(jnp.concatenate([top, halo * inside], axis=0))
    east, west = jnp.maximum(parts[0], 0.0), jnp.maximum(-parts[0], 0.0)
    north, south = jnp.maximum(parts[1], 0.0), jnp.maximum(-parts[1], 0.0)
    keep = 1.0 - east - west - north - south

    def one(layer):
        n, k = layer // 16, lax.rem(layer, 16)
        v = jnp.concatenate(frame(floe[n, k], layer), axis=0)
        for _ in range(NSUB):
            v = (
                v * keep
                + pltpu.roll(v * east, 1, 1)
                + pltpu.roll(v * west, 639, 1)
                + pltpu.roll(v * north, 1, 0)
                + pltpu.roll(v * south, 15, 0)
            )
        out[n, k] = v[0:8, 0:512]

    def pair(i, carry):
        one(2 * i)
        one(2 * i + 1)
        return carry

    lax.fori_loop(0, 40, pair, 0)


def transpose_in(src, table, first, width):
    for lane in range(0, width, 128):
        size = min(128, width - lane)
        block = src[:, :, lane : lane + 128].reshape(N_DEV * 4, 128)
        turned = block.T
        table[first + lane : first + lane + size, :] = turned[:size]


def build_mixing(r, slot, weight, mixing):
    rows = lax.broadcasted_iota(jnp.int32, (N_DEV * 4, 512), 0).astype(jnp.int16)
    total = jnp.zeros((N_DEV * 4, 512), BF16)
    for k in range(4):
        slots = slot[k, pl.ds(r, 1), :].astype(jnp.int16)
        weights = weight[k, pl.ds(r, 1), :].astype(BF16)
        total = total + jnp.where(rows == slots, weights, jnp.zeros((), BF16))
    mixing[r] = total


def wide(column, lanes=4):
    return jnp.concatenate([column] * lanes, axis=1)


def fill_decay(decay, decay_table):
    row = lax.broadcasted_iota(jnp.int32, (72, 128), 0)
    for g in range(18):
        decay_table[g * 72 : g * 72 + 72, :] = jnp.where(row < 36, decay[2 * g], decay[2 * g + 1])


def fill_paths(thick, edge, trig, paths):
    cos_edge, sin_edge = jnp.cos(edge[...]), jnp.sin(edge[...])
    scaled = -math.log2(math.e) * thick[...]
    for r in range(8):
        cosine = wide(trig[0]) * cos_edge[r : r + 1] + wide(trig[1]) * sin_edge[r : r + 1]
        paths[r] = scaled[r : r + 1] / (0.25 + 0.75 * cosine * cosine)


def attenuate(r, steps, table, mixing, decay_table, paths, att):
    path = paths[r]
    for start, size in steps:
        spectrum = jnp.dot(table[start : start + size, :], mixing[r], preferred_element_type=F32)
        decay_rows = wide(decay_table[start : start + size, :])
        first = start % 72
        pieces, have = [path[first:]], 72 - first
        while have < size:
            pieces.append(path)
            have += 72
        factor = jnp.concatenate(pieces, axis=0)[:size]
        att[start : start + size, :] = (spectrum * jnp.exp2(decay_rows * factor)).astype(BF16)


def fracture(hist, weight, ice, brk, out):
    total_w = weight[0] + weight[1] + weight[2] + weight[3]
    used_w = sum(weight[k].astype(BF16).astype(F32) for k in range(4))
    fix = total_w / used_w
    rows = [hist[j] * fix for j in range(16)]
    total = functools.reduce(jnp.add, rows)
    strength = ice[...].astype(F32) * total / (total + 0.005 * 16 * NBIN)
    scale = strength / total
    share = [v * scale for v in rows]
    shorter, run = [], jnp.zeros_like(total)
    for j in range(16):
        shorter.append(run)
        run = run + share[j]
    brk_rows = brk[...]
    for n in range(5):
        above = jnp.zeros_like(total)
        for k in range(15, -1, -1):
            value = out[n, k]
            breakable = jnp.where(brk_rows <= k, value, 0.0)
            out[n, k] = value - breakable * shorter[k] + above * share[k]
            above = above + breakable


STEPS_A = [(i * 144, 144) for i in range(6)] + [(864, 160)]
STEPS_B = [(1024, 128), (1152, 144)]


def kernel(
    decay, floe, courant, spectra, picks, slot, weight, thick, edge, strain, ice, brk, trig, out,
    xa, xb, ra, rb, row_send, row_recv, col_send, col_recv, side,
    table, mixing, decay_table, paths, att, hist,
    send_sem, recv_sem, own_sem, halo_send, halo_recv, group_sem
):
    x, zc, s = coords()
    me = (x * 16 + zc) * 4 + s
    barrier = pltpu.get_barrier_semaphore()
    for i in range(1, 16):
        pl.semaphore_signal(barrier, inc=1, device_id=zc_peer(i, x, zc, s), device_id_type=MESH)
        pl.semaphore_signal(barrier, inc=1, device_id=xy_peer(i, x, zc, s), device_id_type=MESH)
    gather_rows(picks, spectra, xa, xb)
    pl.semaphore_wait(barrier, 30)
    for i in range(1, 16):
        pl.semaphore_signal(group_sem, inc=1, device_id=xy_peer(i, x, zc, s), device_id_type=MESH)
    pack_halo(floe, courant, row_send, col_send)
    pl.semaphore_wait(group_sem, 15)

    halo = halo_copies(row_send, row_recv, col_send, col_recv, halo_send, halo_recv)
    for copy in halo:
        copy.start()
    own = [
        pltpu.make_async_copy(xa.at[me], ra.at[me], own_sem.at[0]),
        pltpu.make_async_copy(xb.at[me], rb.at[me], own_sem.at[1]),
    ]
    for copy in own:
        copy.start()
    send_all(xa, ra, send_sem.at[0], recv_sem.at[0])
    send_all(xb, rb, send_sem.at[1], recv_sem.at[1])

    fill_decay(decay, decay_table)
    fill_paths(thick, edge, trig, paths)

    def mix_row(r, carry):
        build_mixing(r, slot, weight, mixing)
        return carry

    lax.fori_loop(0, 8, mix_row, 0)
    for copy in halo:
        copy.wait()
    unpack_columns(col_recv, side)
    transport(floe, courant, row_recv, side, out)

    others = pl.ds(0, N_DEV - 1)
    own[0].wait()
    pltpu.make_async_copy(xa.at[others], ra.at[others], recv_sem.at[0]).wait()
    transpose_in(ra, table, 0, SPLIT)

    def row_a(r, carry):
        attenuate(r, STEPS_A, table, mixing, decay_table, paths, att)
        part = jnp.dot(strain[:, :SPLIT], att[:SPLIT], preferred_element_type=F32)
        hist[:, pl.ds(r, 1), :] = part[:, None, :]
        return carry

    lax.fori_loop(0, 8, row_a, 0)
    own[1].wait()
    pltpu.make_async_copy(xb.at[others], rb.at[others], recv_sem.at[1]).wait()
    transpose_in(rb, table, SPLIT, NBIN - SPLIT)

    def row_b(r, carry):
        attenuate(r, STEPS_B, table, mixing, decay_table, paths, att)
        part = jnp.dot(strain[:, SPLIT:], att[SPLIT:], preferred_element_type=F32)
        hist[:, pl.ds(r, 1), :] += part[:, None, :]
        return carry

    lax.fori_loop(0, 8, row_b, 0)
    fracture(hist, weight, ice, brk, out)
    pltpu.make_async_copy(xa.at[others], ra.at[others], send_sem.at[0]).wait()
    pltpu.make_async_copy(xb.at[others], rb.at[others], send_sem.at[1]).wait()


def shards(
    floe_area, courant, spectra, send_rows, src_slot, src_weight, thickness, edge_angle,
    decay_rate, strain_table, ice_mask, break_bin
):
    angles = 2.0 * math.pi * np.tile(np.arange(NDIR), 2) / NDIR - math.pi
    trig = np.stack([np.cos(angles), np.sin(angles)]).astype(np.float32)
    trig = jnp.asarray(np.broadcast_to(trig[:, :, None], (2, 72, 128)))
    vmem = pl.BlockSpec(memory_space=pltpu.VMEM)
    return pl.pallas_call(
        kernel,
        out_shape=jax.ShapeDtypeStruct(floe_area.shape, F32),
        in_specs=[pl.BlockSpec(memory_space=pltpu.SMEM)] + [vmem] * 12,
        out_specs=vmem,
        scratch_shapes=[
            pltpu.VMEM((N_DEV, 4, SPLIT), BF16),
            pltpu.VMEM((N_DEV, 4, TAIL), BF16),
            pltpu.VMEM((N_DEV, 4, SPLIT), BF16),
            pltpu.VMEM((N_DEV, 4, TAIL), BF16),
            pltpu.VMEM((2, 82, 4, 512), F32),
            pltpu.VMEM((2, 82, 4, 512), F32),
            pltpu.VMEM((2, 8, COLUMN_ROWS), F32),
            pltpu.VMEM((2, 3, 8, COLUMN_ROWS), F32),
            pltpu.VMEM((3, COLUMN_ROWS, 128), F32),
            pltpu.VMEM((NBIN, N_DEV * 4), BF16),
            pltpu.VMEM((8, N_DEV * 4, 512), BF16),
            pltpu.VMEM((NBIN, 128), F32),
            pltpu.VMEM((8, 72, 512), F32),
            pltpu.VMEM((NBIN, 512), BF16),
            pltpu.VMEM((16, 8, 512), F32),
            pltpu.SemaphoreType.DMA((2,)),
            pltpu.SemaphoreType.DMA((2,)),
            pltpu.SemaphoreType.DMA((2,)),
            pltpu.SemaphoreType.DMA((8,)),
            pltpu.SemaphoreType.DMA((8,)),
            pltpu.SemaphoreType.REGULAR,
        ],
        compiler_params=pltpu.CompilerParams(
            collective_id=0, has_side_effects=True, vmem_limit_bytes=56 << 20
        ),
    )(
        decay_rate, floe_area, courant, spectra[0, 0], send_rows[0, 0], src_slot, src_weight,
        thickness, edge_angle, strain_table, ice_mask, break_bin, trig
    )


def solution(mesh):
    in_specs = (
        P(None, None, "sub", "tiles"),
        P(None, "sub", "tiles"),
        P("tiles", "sub", None, None),
        P("tiles", "sub", None, None, None),
        P(None, "sub", "tiles"),
        P(None, "sub", "tiles"),
        P("sub", "tiles"),
        P("sub", "tiles"),
        P(),
        P(),
        P("sub", "tiles"),
        P("sub", "tiles"),
    )
    out_specs = P(None, None, "sub", "tiles")
    return jax.shard_map(shards, mesh=mesh, in_specs=in_specs, out_specs=out_specs, check_vma=False)
```

```python
import functools
import math

import jax
import jax.numpy as jnp
from jax import lax
from jax.experimental import pallas as pl
from jax.experimental.pallas import tpu as pltpu
from jax.sharding import PartitionSpec as P

MESH = pl.DeviceIdType.MESH
F32 = jnp.float32
BF16 = jnp.bfloat16
NDIR = 36
NBIN = 1296
NSUB = 3
N_DEV = 256
SPLIT = 1024
TAIL = 256
WIDE = SPLIT + TAIL
COLUMN_ROWS = 768


def coords():
    t, s = lax.axis_index("tiles"), lax.axis_index("sub")
    return t // 16, lax.rem(t, 16), s


def zc_peer(i, x, zc, s):
    c = lax.rem(lax.rem(zc, 2) + i % 2, 2)
    z = lax.rem(zc // 2 + i // 2, 8)
    return (x * 16 + z * 2 + c, s)


def xy_peer(i, x, zc, s):
    return (lax.rem(x + i // 4, 4) * 16 + zc, lax.rem(s + i % 4, 4))


def tile_of(x, zc, dx, dz, dc):
    core = lax.rem(lax.rem(zc, 2) + dc, 2)
    return lax.rem(x + dx, 4) * 16 + lax.rem(zc // 2 + dz, 8) * 2 + core


def send_all(src, dst, send_sem, recv_sem):
    x, zc, s = coords()
    me = (zc * 4 + x) * 4 + s

    def one(i, carry):
        tile = tile_of(x, zc, i // 64, lax.rem(i // 2, 8), lax.rem(i, 2))
        sub = lax.rem(s + lax.rem(i // 16, 4), 4)
        pltpu.make_async_remote_copy(
            src_ref=src.at[tile * 4 + sub],
            dst_ref=dst.at[me],
            send_sem=send_sem,
            recv_sem=recv_sem,
            device_id=(tile, sub),
            device_id_type=MESH,
        ).start()
        return carry

    lax.fori_loop(1, N_DEV, one, 0)


def send_group(peer, number, src, dst, me, send_sem, recv_sem):
    x, zc, s = coords()
    for i in range(1, 16):
        device = peer(i, x, zc, s)
        pltpu.make_async_remote_copy(
            src_ref=src.at[number(device)],
            dst_ref=dst.at[me],
            send_sem=send_sem,
            recv_sem=recv_sem,
            device_id=device,
            device_id_type=MESH,
        ).start()


def choose_cells(picks, choose):
    pick = picks[...].reshape(16, 64).astype(F32)
    pick = jnp.concatenate([pick, jnp.zeros((16, 64), F32)], axis=1).T[:64]
    pick = jnp.broadcast_to(pick.reshape(64, 1, 16), (64, 16, 16)).reshape(N_DEV * 4, 16)
    row = lax.broadcasted_iota(jnp.int32, (N_DEV * 4, 16), 0)
    lane = lax.broadcasted_iota(jnp.int32, (N_DEV * 4, 16), 1)
    column = jnp.sum(jnp.where(lane == lax.rem(row, 16), pick, 0.0), axis=1, keepdims=True)
    cell = lax.broadcasted_iota(jnp.int32, (N_DEV * 4, 512), 1)
    choose[...] = jnp.where(cell == column.astype(jnp.int32), 1.0, 0.0).astype(BF16)


def gather_rows(choose, spectra, xa, xb, tail_send):
    over_cells = (((1,), (1,)), ((), ()))
    for start in range(0, WIDE, 256):
        rows = lax.dot_general(
            choose[...], spectra[start : start + 256, :], over_cells, preferred_element_type=F32
        )
        rows = rows.astype(BF16).reshape(N_DEV, 4, 256)
        if start < SPLIT:
            xa[:, :, start : start + 256] = rows
        else:
            xb[...] = rows
    last = lax.dot_general(
        choose[...], spectra[WIDE:, :], over_cells, preferred_element_type=F32
    )
    filler = jnp.zeros((64, NBIN - WIDE), F32)
    for zc in range(16):
        pieces = [last[(x * 16 + zc) * 16 : (x * 16 + zc) * 16 + 16] for x in range(4)]
        tail_send[zc] = jnp.concatenate(pieces + [filler], axis=0).T.astype(BF16)


def regroup_tail(tail_mid, tail_pass):
    turned = tail_mid[...].reshape(256, 128).T
    tail_pass[...] = turned[:64].reshape(16, 4, 256)


def finish_tail(tail_recv, table):
    turned = tail_recv[...].reshape(64, 256).T
    for zc in range(0, 16, 2):
        both = jnp.concatenate(
            [turned[zc * 16 : zc * 16 + 16], turned[zc * 16 + 16 : zc * 16 + 32]], axis=1
        )
        table[WIDE:, zc * 64 : zc * 64 + 128] = both


def pack_halo(floe, courant, row_send, col_send):
    for n in range(5):
        row_send[0, n * 16 : n * 16 + 16] = floe[n, :, 0:4, :]
        row_send[1, n * 16 : n * 16 + 16] = floe[n, :, 4:8, :]
    row_send[0, 80:82] = courant[:, 0:4, :]
    row_send[1, 80:82] = courant[:, 4:8, :]
    filler = jnp.zeros((COLUMN_ROWS - 656, 128), F32)
    for side, lanes in ((0, slice(0, 128)), (1, slice(384, 512))):
        strip = jnp.concatenate(
            [floe[:, :, :, lanes].reshape(640, 128), courant[:, :, lanes].reshape(16, 128), filler]
        )
        turned = strip.T
        col_send[side] = turned[0:8] if side == 0 else turned[120:128]


def halo_copies(row_send, row_recv, col_send, col_recv, send_sem, recv_sem):
    t, s = lax.axis_index("tiles"), lax.axis_index("sub")
    n_tiles = lax.axis_size("tiles")
    copies = []

    def add(src, dst, device):
        k = len(copies)
        copies.append(
            pltpu.make_async_remote_copy(
                src_ref=src,
                dst_ref=dst,
                send_sem=send_sem.at[k],
                recv_sem=recv_sem.at[k],
                device_id=device,
                device_id_type=MESH,
            )
        )

    for side, step in ((0, n_tiles - 1), (1, 1)):
        for group, shift in ((0, 0), (1, 3), (2, 1)):
            device = (lax.rem(t + step, n_tiles), lax.rem(s + shift, 4))
            add(col_send.at[side], col_recv.at[side, group], device)
    add(row_send.at[0], row_recv.at[0], (t, lax.rem(s + 3, 4)))
    add(row_send.at[1], row_recv.at[1], (t, lax.rem(s + 1, 4)))
    return copies


def unpack_columns(col_recv, side):
    for group in range(3):
        side[group] = jnp.concatenate(
            [col_recv[0, group], jnp.zeros((112, COLUMN_ROWS), F32), col_recv[1, group]], axis=0
        ).T


def transport(floe, courant, row_recv, side, out):
    s = lax.axis_index("sub")
    row = lax.broadcasted_iota(jnp.int32, (8, 128), 0)

    def frame(own, layer):
        start = layer * 8 if isinstance(layer, int) else pl.multiple_of(layer * 8, 8)
        here = pl.ds(start, 8)
        corner = jnp.where(row < 4, side[1, here], side[2, here])
        top = jnp.concatenate([own, side[0, here]], axis=1)
        halo = jnp.concatenate([row_recv[0, layer], row_recv[1, layer]], axis=0)
        return top, jnp.concatenate([halo, corner], axis=1)

    wide_row = lax.broadcasted_iota(jnp.int32, (8, 640), 0)
    after, before = jnp.where(s < 3, 1.0, 0.0), jnp.where(s > 0, 1.0, 0.0)
    inside = jnp.where(wide_row < 4, after, before)
    parts = []
    for k in range(2):
        top, halo = frame(courant[k], 80 + k)
        parts.append(jnp.concatenate([top, halo * inside], axis=0))
    east, west = jnp.maximum(parts[0], 0.0), jnp.maximum(-parts[0], 0.0)
    north, south = jnp.maximum(parts[1], 0.0), jnp.maximum(-parts[1], 0.0)
    keep = 1.0 - east - west - north - south

    def one(layer):
        n, k = layer // 16, lax.rem(layer, 16)
        v = jnp.concatenate(frame(floe[n, k], layer), axis=0)
        for _ in range(NSUB):
            v = (
                v * keep
                + pltpu.roll(v * east, 1, 1)
                + pltpu.roll(v * west, 639, 1)
                + pltpu.roll(v * north, 1, 0)
                + pltpu.roll(v * south, 15, 0)
            )
        out[n, k] = v[0:8, 0:512]

    def pair(i, carry):
        one(2 * i)
        one(2 * i + 1)
        return carry

    lax.fori_loop(0, 40, pair, 0)


def transpose_in(src, table, first, width):
    for lane in range(0, width, 128):
        size = min(128, width - lane)
        block = src[:, :, lane : lane + 128].reshape(N_DEV * 4, 128)
        turned = block.T
        table[first + lane : first + lane + size, :] = turned[:size]


def build_mixing(r, slot, weight, mixing):
    rows = lax.broadcasted_iota(jnp.int32, (N_DEV * 4, 512), 0).astype(jnp.int16)
    total = jnp.zeros((N_DEV * 4, 512), BF16)
    for k in range(4):
        given = slot[k, pl.ds(r, 1), :]
        slots = lax.rem(given // 16, 16) * 64 + given // 256 * 16 + lax.rem(given, 16)
        slots = slots.astype(jnp.int16)
        weights = weight[k, pl.ds(r, 1), :].astype(BF16)
        total = total + jnp.where(rows == slots, weights, jnp.zeros((), BF16))
    mixing[r] = total


def wide(column, lanes=4):
    return jnp.concatenate([column] * lanes, axis=1)


def fill_decay(decay, decay_table):
    row = lax.broadcasted_iota(jnp.int32, (72, 128), 0)
    for g in range(18):
        decay_table[g * 72 : g * 72 + 72, :] = jnp.where(row < 36, decay[2 * g], decay[2 * g + 1])


def fill_paths(thick, edge, paths):
    direction = lax.rem(lax.broadcasted_iota(jnp.int32, (72, 128), 0), NDIR).astype(F32)
    angle = 2.0 * math.pi * direction / NDIR - math.pi
    trig = (jnp.cos(angle), jnp.sin(angle))
    cos_edge, sin_edge = jnp.cos(edge[...]), jnp.sin(edge[...])
    scaled = -math.log2(math.e) * thick[...]
    for r in range(8):
        cosine = wide(trig[0]) * cos_edge[r : r + 1] + wide(trig[1]) * sin_edge[r : r + 1]
        paths[r] = scaled[r : r + 1] / (0.25 + 0.75 * cosine * cosine)


def attenuate(r, steps, table, mixing, decay_table, paths, att):
    path = paths[r]
    for start, size in steps:
        spectrum = jnp.dot(table[start : start + size, :], mixing[r], preferred_element_type=F32)
        decay_rows = wide(decay_table[start : start + size, :])
        first = start % 72
        pieces, have = [path[first:]], 72 - first
        while have < size:
            pieces.append(path)
            have += 72
        factor = jnp.concatenate(pieces, axis=0)[:size]
        att[start : start + size, :] = (spectrum * jnp.exp2(decay_rows * factor)).astype(BF16)


def fracture(hist, weight, ice, brk, out):
    total_w = weight[0] + weight[1] + weight[2] + weight[3]
    used_w = sum(weight[k].astype(BF16).astype(F32) for k in range(4))
    fix = total_w / used_w
    rows = [hist[j] * fix for j in range(16)]
    total = functools.reduce(jnp.add, rows)
    strength = ice[...].astype(F32) * total / (total + 0.005 * 16 * NBIN)
    scale = strength / total
    share = [v * scale for v in rows]
    shorter, run = [], jnp.zeros_like(total)
    for j in range(16):
        shorter.append(run)
        run = run + share[j]
    brk_rows = brk[...]
    for n in range(5):
        above = jnp.zeros_like(total)
        for k in range(15, -1, -1):
            value = out[n, k]
            breakable = jnp.where(brk_rows <= k, value, 0.0)
            out[n, k] = value - breakable * shorter[k] + above * share[k]
            above = above + breakable


STEPS_A = [(i * 144, 144) for i in range(6)] + [(864, 160)]
STEPS_B = [(1024, 128), (1152, 144)]


def kernel(
    decay, floe_hbm, courant_hbm, spectra_hbm, picks_hbm, slot_hbm, weight_hbm, thick_hbm, edge_hbm,
    strain_hbm, ice_hbm, brk_hbm, out,
    floe, courant, spectra, picks, slot, weight, thick, edge, strain, ice, brk,
    choose, xa, xb, ra, rb, tail_send, tail_mid, tail_pass, tail_recv,
    row_send, row_recv, col_send, col_recv, side,
    table, mixing, decay_table, paths, att, hist,
    load_sem, send_sem, recv_sem, own_sem, halo_send, halo_recv, group_sem
):
    x, zc, s = coords()
    me = (x * 16 + zc) * 4 + s
    me_slot = (zc * 4 + x) * 4 + s
    barrier = pltpu.get_barrier_semaphore()
    for i in range(1, 16):
        pl.semaphore_signal(barrier, inc=1, device_id=zc_peer(i, x, zc, s), device_id_type=MESH)
        pl.semaphore_signal(barrier, inc=1, device_id=xy_peer(i, x, zc, s), device_id_type=MESH)
    pairs = (
        (picks_hbm, picks), (spectra_hbm, spectra), (floe_hbm, floe), (courant_hbm, courant),
        (slot_hbm, slot), (weight_hbm, weight), (thick_hbm, thick), (edge_hbm, edge),
        (strain_hbm, strain), (ice_hbm, ice), (brk_hbm, brk),
    )
    loads = [
        pltpu.make_async_copy(src, dst, load_sem.at[k]) for k, (src, dst) in enumerate(pairs)
    ]
    for copy in loads:
        copy.start()
    loads[0].wait()
    choose_cells(picks, choose)
    pl.semaphore_wait(barrier, 30)
    for i in range(1, 16):
        pl.semaphore_signal(group_sem, inc=1, device_id=xy_peer(i, x, zc, s), device_id_type=MESH)
    loads[1].wait()
    gather_rows(choose, spectra, xa, xb, tail_send)
    for copy in loads[2:]:
        copy.wait()
    pack_halo(floe, courant, row_send, col_send)
    pl.semaphore_wait(group_sem, 15)

    def zc_number(device):
        return lax.rem(device[0], 16)

    def xy_number(device):
        return device[0] // 16 * 4 + device[1]

    halo = halo_copies(row_send, row_recv, col_send, col_recv, halo_send, halo_recv)
    for copy in halo:
        copy.start()
    own = [
        pltpu.make_async_copy(xa.at[me], ra.at[me_slot], own_sem.at[0]),
        pltpu.make_async_copy(xb.at[me], rb.at[me_slot], own_sem.at[1]),
        pltpu.make_async_copy(tail_send.at[zc], tail_mid.at[zc], own_sem.at[2]),
    ]
    for copy in own:
        copy.start()
    send_group(zc_peer, zc_number, tail_send, tail_mid, zc, send_sem.at[2], recv_sem.at[2])
    send_all(xa, ra, send_sem.at[0], recv_sem.at[0])
    send_all(xb, rb, send_sem.at[1], recv_sem.at[1])

    fifteen = pl.ds(0, 15)
    own[2].wait()
    pltpu.make_async_copy(tail_send.at[fifteen], tail_mid.at[fifteen], recv_sem.at[2]).wait()
    regroup_tail(tail_mid, tail_pass)
    own_tail = pltpu.make_async_copy(
        tail_pass.at[x * 4 + s], tail_recv.at[x * 4 + s], own_sem.at[3]
    )
    own_tail.start()
    send_group(xy_peer, xy_number, tail_pass, tail_recv, x * 4 + s, send_sem.at[3], recv_sem.at[3])

    fill_decay(decay, decay_table)
    fill_paths(thick, edge, paths)

    def mix_row(r, carry):
        build_mixing(r, slot, weight, mixing)
        return carry

    lax.fori_loop(0, 8, mix_row, 0)
    for copy in halo:
        copy.wait()
    unpack_columns(col_recv, side)
    transport(floe, courant, row_recv, side, out)

    own_tail.wait()
    pltpu.make_async_copy(tail_pass.at[fifteen], tail_recv.at[fifteen], recv_sem.at[3]).wait()
    finish_tail(tail_recv, table)

    others = pl.ds(0, N_DEV - 1)
    own[0].wait()
    pltpu.make_async_copy(xa.at[others], ra.at[others], recv_sem.at[0]).wait()
    transpose_in(ra, table, 0, SPLIT)

    def row_a(r, carry):
        attenuate(r, STEPS_A, table, mixing, decay_table, paths, att)
        part = jnp.dot(strain[:, :SPLIT], att[:SPLIT], preferred_element_type=F32)
        hist[:, pl.ds(r, 1), :] = part[:, None, :]
        return carry

    lax.fori_loop(0, 8, row_a, 0)
    own[1].wait()
    pltpu.make_async_copy(xb.at[others], rb.at[others], recv_sem.at[1]).wait()
    transpose_in(rb, table, SPLIT, TAIL)

    def row_b(r, carry):
        attenuate(r, STEPS_B, table, mixing, decay_table, paths, att)
        part = jnp.dot(strain[:, SPLIT:], att[SPLIT:], preferred_element_type=F32)
        hist[:, pl.ds(r, 1), :] += part[:, None, :]
        return carry

    lax.fori_loop(0, 8, row_b, 0)
    fracture(hist, weight, ice, brk, out)
    pltpu.make_async_copy(xa.at[others], ra.at[others], send_sem.at[0]).wait()
    pltpu.make_async_copy(xb.at[others], rb.at[others], send_sem.at[1]).wait()
    pltpu.make_async_copy(tail_send.at[fifteen], tail_mid.at[fifteen], send_sem.at[2]).wait()
    pltpu.make_async_copy(tail_pass.at[fifteen], tail_recv.at[fifteen], send_sem.at[3]).wait()


def shards(
    floe_area, courant, spectra, send_rows, src_slot, src_weight, thickness, edge_angle,
    decay_rate, strain_table, ice_mask, break_bin
):
    operands = (
        floe_area, courant, spectra[0, 0].T, jnp.transpose(send_rows[0, 0], (1, 2, 0)), src_slot,
        src_weight, thickness, edge_angle, strain_table, ice_mask, break_bin
    )
    vmem = pl.BlockSpec(memory_space=pltpu.VMEM)
    return pl.pallas_call(
        kernel,
        out_shape=jax.ShapeDtypeStruct(floe_area.shape, F32),
        in_specs=[pl.BlockSpec(memory_space=pltpu.SMEM)]
        + [pl.BlockSpec(memory_space=pl.ANY)] * len(operands),
        out_specs=vmem,
        scratch_shapes=[pltpu.VMEM(v.shape, v.dtype) for v in operands]
        + [
            pltpu.VMEM((N_DEV * 4, 512), BF16),
            pltpu.VMEM((N_DEV, 4, SPLIT), BF16),
            pltpu.VMEM((N_DEV, 4, TAIL), BF16),
            pltpu.VMEM((N_DEV, 4, SPLIT), BF16),
            pltpu.VMEM((N_DEV, 4, TAIL), BF16),
            pltpu.VMEM((16, 16, 128), BF16),
            pltpu.VMEM((16, 16, 128), BF16),
            pltpu.VMEM((16, 4, 256), BF16),
            pltpu.VMEM((16, 4, 256), BF16),
            pltpu.VMEM((2, 82, 4, 512), F32),
            pltpu.VMEM((2, 82, 4, 512), F32),
            pltpu.VMEM((2, 8, COLUMN_ROWS), F32),
            pltpu.VMEM((2, 3, 8, COLUMN_ROWS), F32),
            pltpu.VMEM((3, COLUMN_ROWS, 128), F32),
            pltpu.VMEM((NBIN, N_DEV * 4), BF16),
            pltpu.VMEM((8, N_DEV * 4, 512), BF16),
            pltpu.VMEM((NBIN, 128), F32),
            pltpu.VMEM((8, 72, 512), F32),
            pltpu.VMEM((NBIN, 512), BF16),
            pltpu.VMEM((16, 8, 512), F32),
            pltpu.SemaphoreType.DMA((len(operands),)),
            pltpu.SemaphoreType.DMA((4,)),
            pltpu.SemaphoreType.DMA((4,)),
            pltpu.SemaphoreType.DMA((4,)),
            pltpu.SemaphoreType.DMA((8,)),
            pltpu.SemaphoreType.DMA((8,)),
            pltpu.SemaphoreType.REGULAR,
        ],
        compiler_params=pltpu.CompilerParams(
            collective_id=0, has_side_effects=True, vmem_limit_bytes=56 << 20
        ),
    )(decay_rate, *operands)


def solution(mesh):
    in_specs = (
        P(None, None, "sub", "tiles"),
        P(None, "sub", "tiles"),
        P("tiles", "sub", None, None),
        P("tiles", "sub", None, None, None),
        P(None, "sub", "tiles"),
        P(None, "sub", "tiles"),
        P("sub", "tiles"),
        P("sub", "tiles"),
        P(),
        P(),
        P("sub", "tiles"),
        P("sub", "tiles"),
    )
    out_specs = P(None, None, "sub", "tiles")
    return jax.shard_map(shards, mesh=mesh, in_specs=in_specs, out_specs=out_specs, check_vma=False)
```

```python
import functools
import math

import jax
import jax.numpy as jnp
from jax import lax
from jax.experimental import pallas as pl
from jax.experimental.pallas import tpu as pltpu
from jax.sharding import PartitionSpec as P

MESH = pl.DeviceIdType.MESH
F32 = jnp.float32
BF16 = jnp.bfloat16
NDIR = 36
NBIN = 1296
NSUB = 3
N_DEV = 256
RANGES = ((0, 768), (768, 384), (1152, 128))
WIDE = 1280
COLUMN_ROWS = 768


def coords():
    t, s = lax.axis_index("tiles"), lax.axis_index("sub")
    return t // 16, lax.rem(t, 16), s


def zc_peer(i, x, zc, s):
    c = lax.rem(lax.rem(zc, 2) + i % 2, 2)
    z = lax.rem(zc // 2 + i // 2, 8)
    return (x * 16 + z * 2 + c, s)


def xy_peer(i, x, zc, s):
    return (lax.rem(x + i // 4, 4) * 16 + zc, lax.rem(s + i % 4, 4))


def zc_numbers(zc):
    return [
        lax.rem(zc // 2 + i // 2, 8) * 2 + lax.rem(lax.rem(zc, 2) + i % 2, 2) for i in range(16)
    ]


def sender(src, dst, send_sem, recv_sem):
    x, zc, s = coords()
    me = (zc * 4 + x) * 4 + s
    numbers = zc_numbers(zc)

    def send(tile, sub):
        pltpu.make_async_remote_copy(
            src_ref=src.at[tile * 4 + sub],
            dst_ref=dst.at[me],
            send_sem=send_sem,
            recv_sem=recv_sem,
            device_id=(tile, sub),
            device_id_type=MESH,
        ).start()

    def near():
        for number in numbers[1:]:
            send(x * 16 + number, s)

        def one(i, carry):
            send(lax.rem(x + i // 4, 4) * 16 + zc, lax.rem(s + lax.rem(i, 4), 4))
            return carry

        lax.fori_loop(1, 16, one, 0)

    def far():
        def one(i, carry):
            first = lax.rem(x + i // 4, 4) * 16
            sub = lax.rem(s + lax.rem(i, 4), 4)
            for number in numbers[1:]:
                send(first + number, sub)
            return carry

        lax.fori_loop(1, 16, one, 0)

    return near, far


def send_group(peer, number, src, dst, me, send_sem, recv_sem):
    x, zc, s = coords()
    for i in range(1, 16):
        device = peer(i, x, zc, s)
        pltpu.make_async_remote_copy(
            src_ref=src.at[number(device)],
            dst_ref=dst.at[me],
            send_sem=send_sem,
            recv_sem=recv_sem,
            device_id=device,
            device_id_type=MESH,
        ).start()


def choose_cells(picks, choose):
    pick = picks[...].reshape(16, 64).astype(F32)
    pick = jnp.concatenate([pick, jnp.zeros((16, 64), F32)], axis=1).T[:64]
    pick = jnp.broadcast_to(pick.reshape(64, 1, 16), (64, 16, 16)).reshape(N_DEV * 4, 16)
    row = lax.broadcasted_iota(jnp.int32, (N_DEV * 4, 16), 0)
    lane = lax.broadcasted_iota(jnp.int32, (N_DEV * 4, 16), 1)
    column = jnp.sum(jnp.where(lane == lax.rem(row, 16), pick, 0.0), axis=1, keepdims=True)
    cell = lax.broadcasted_iota(jnp.int32, (N_DEV * 4, 512), 1)
    choose[...] = jnp.where(cell == column.astype(jnp.int32), 1.0, 0.0).astype(BF16)


OVER_CELLS = (((1,), (1,)), ((), ()))


def gather_rows(choose, spectra, first, size, dst):
    for lane in range(0, size, 256):
        width = min(256, size - lane)
        start = first + lane
        rows = lax.dot_general(
            choose[...], spectra[start : start + width, :], OVER_CELLS, preferred_element_type=F32
        )
        dst[:, :, lane : lane + width] = rows.astype(BF16).reshape(N_DEV, 4, width)


def gather_tail(choose, spectra, tail_send):
    last = lax.dot_general(
        choose[...], spectra[WIDE:, :], OVER_CELLS, preferred_element_type=F32
    )
    filler = jnp.zeros((64, NBIN - WIDE), F32)
    for zc in range(16):
        pieces = [last[(x * 16 + zc) * 16 : (x * 16 + zc) * 16 + 16] for x in range(4)]
        tail_send[zc] = jnp.concatenate(pieces + [filler], axis=0).T.astype(BF16)


def regroup_tail(tail_mid, tail_pass):
    turned = tail_mid[...].reshape(256, 128).T
    tail_pass[...] = turned[:64].reshape(16, 4, 256)


def finish_tail(tail_recv, table):
    turned = tail_recv[...].reshape(64, 256).T
    for zc in range(0, 16, 2):
        both = jnp.concatenate(
            [turned[zc * 16 : zc * 16 + 16], turned[zc * 16 + 16 : zc * 16 + 32]], axis=1
        )
        table[WIDE:, zc * 64 : zc * 64 + 128] = both


def pack_halo(floe, courant, row_send, col_send):
    for n in range(5):
        row_send[0, n * 16 : n * 16 + 16] = floe[n, :, 0:4, :]
        row_send[1, n * 16 : n * 16 + 16] = floe[n, :, 4:8, :]
    row_send[0, 80:82] = courant[:, 0:4, :]
    row_send[1, 80:82] = courant[:, 4:8, :]
    filler = jnp.zeros((COLUMN_ROWS - 656, 128), F32)
    for side, lanes in ((0, slice(0, 128)), (1, slice(384, 512))):
        strip = jnp.concatenate(
            [floe[:, :, :, lanes].reshape(640, 128), courant[:, :, lanes].reshape(16, 128), filler]
        )
        turned = strip.T
        col_send[side] = turned[0:8] if side == 0 else turned[120:128]


def halo_copies(row_send, row_recv, col_send, col_recv, send_sem, recv_sem):
    t, s = lax.axis_index("tiles"), lax.axis_index("sub")
    n_tiles = lax.axis_size("tiles")
    copies = []

    def add(src, dst, device):
        k = len(copies)
        copies.append(
            pltpu.make_async_remote_copy(
                src_ref=src,
                dst_ref=dst,
                send_sem=send_sem.at[k],
                recv_sem=recv_sem.at[k],
                device_id=device,
                device_id_type=MESH,
            )
        )

    for side, step in ((0, n_tiles - 1), (1, 1)):
        for group, shift in ((0, 0), (1, 3), (2, 1)):
            device = (lax.rem(t + step, n_tiles), lax.rem(s + shift, 4))
            add(col_send.at[side], col_recv.at[side, group], device)
    add(row_send.at[0], row_recv.at[0], (t, lax.rem(s + 3, 4)))
    add(row_send.at[1], row_recv.at[1], (t, lax.rem(s + 1, 4)))
    return copies


def unpack_columns(col_recv, side):
    for group in range(3):
        side[group] = jnp.concatenate(
            [col_recv[0, group], jnp.zeros((112, COLUMN_ROWS), F32), col_recv[1, group]], axis=0
        ).T


def transport(floe, courant, row_recv, side, out):
    s = lax.axis_index("sub")
    row = lax.broadcasted_iota(jnp.int32, (8, 128), 0)

    def frame(own, layer):
        start = layer * 8 if isinstance(layer, int) else pl.multiple_of(layer * 8, 8)
        here = pl.ds(start, 8)
        corner = jnp.where(row < 4, side[1, here], side[2, here])
        top = jnp.concatenate([own, side[0, here]], axis=1)
        halo = jnp.concatenate([row_recv[0, layer], row_recv[1, layer]], axis=0)
        return top, jnp.concatenate([halo, corner], axis=1)

    wide_row = lax.broadcasted_iota(jnp.int32, (8, 640), 0)
    after, before = jnp.where(s < 3, 1.0, 0.0), jnp.where(s > 0, 1.0, 0.0)
    inside = jnp.where(wide_row < 4, after, before)
    parts = []
    for k in range(2):
        top, halo = frame(courant[k], 80 + k)
        parts.append(jnp.concatenate([top, halo * inside], axis=0))
    east, west = jnp.maximum(parts[0], 0.0), jnp.maximum(-parts[0], 0.0)
    north, south = jnp.maximum(parts[1], 0.0), jnp.maximum(-parts[1], 0.0)
    keep = 1.0 - east - west - north - south

    def one(layer):
        n, k = layer // 16, lax.rem(layer, 16)
        v = jnp.concatenate(frame(floe[n, k], layer), axis=0)
        for _ in range(NSUB):
            v = (
                v * keep
                + pltpu.roll(v * east, 1, 1)
                + pltpu.roll(v * west, 639, 1)
                + pltpu.roll(v * north, 1, 0)
                + pltpu.roll(v * south, 15, 0)
            )
        out[n, k] = v[0:8, 0:512]

    def pair(i, carry):
        one(2 * i)
        one(2 * i + 1)
        return carry

    lax.fori_loop(0, 40, pair, 0)


def transpose_in(src, table, first, width):
    for lane in range(0, width, 128):
        size = min(128, width - lane)
        block = src[:, :, lane : lane + 128].reshape(N_DEV * 4, 128)
        turned = block.T
        table[first + lane : first + lane + size, :] = turned[:size]


def build_mixing(r, slot, weight, mixing):
    rows = lax.broadcasted_iota(jnp.int32, (N_DEV * 4, 512), 0).astype(jnp.int16)
    total = jnp.zeros((N_DEV * 4, 512), BF16)
    for k in range(4):
        given = slot[k, pl.ds(r, 1), :]
        slots = lax.rem(given // 16, 16) * 64 + given // 256 * 16 + lax.rem(given, 16)
        slots = slots.astype(jnp.int16)
        weights = weight[k, pl.ds(r, 1), :].astype(BF16)
        total = total + jnp.where(rows == slots, weights, jnp.zeros((), BF16))
    mixing[r] = total


def wide(column, lanes=4):
    return jnp.concatenate([column] * lanes, axis=1)


def fill_decay(decay, decay_table):
    row = lax.broadcasted_iota(jnp.int32, (72, 128), 0)
    for g in range(18):
        decay_table[g * 72 : g * 72 + 72, :] = jnp.where(row < 36, decay[2 * g], decay[2 * g + 1])


def fill_paths(thick, edge, paths):
    direction = lax.rem(lax.broadcasted_iota(jnp.int32, (72, 128), 0), NDIR).astype(F32)
    angle = 2.0 * math.pi * direction / NDIR - math.pi
    trig = (jnp.cos(angle), jnp.sin(angle))
    cos_edge, sin_edge = jnp.cos(edge[...]), jnp.sin(edge[...])
    scaled = -math.log2(math.e) * thick[...]
    for r in range(8):
        cosine = wide(trig[0]) * cos_edge[r : r + 1] + wide(trig[1]) * sin_edge[r : r + 1]
        paths[r] = scaled[r : r + 1] / (0.25 + 0.75 * cosine * cosine)


def attenuate(r, steps, table, mixing, decay_table, paths, att):
    path = paths[r]
    for start, size in steps:
        spectrum = jnp.dot(table[start : start + size, :], mixing[r], preferred_element_type=F32)
        decay_rows = wide(decay_table[start : start + size, :])
        first = start % 72
        pieces, have = [path[first:]], 72 - first
        while have < size:
            pieces.append(path)
            have += 72
        factor = jnp.concatenate(pieces, axis=0)[:size]
        att[start : start + size, :] = (spectrum * jnp.exp2(decay_rows * factor)).astype(BF16)


def fracture(hist, weight, ice, brk, out):
    total_w = weight[0] + weight[1] + weight[2] + weight[3]
    used_w = sum(weight[k].astype(BF16).astype(F32) for k in range(4))
    fix = total_w / used_w
    rows = [hist[j] * fix for j in range(16)]
    total = functools.reduce(jnp.add, rows)
    strength = ice[...].astype(F32) * total / (total + 0.005 * 16 * NBIN)
    scale = strength / total
    share = [v * scale for v in rows]
    shorter, run = [], jnp.zeros_like(total)
    for j in range(16):
        shorter.append(run)
        run = run + share[j]
    brk_rows = brk[...]
    for n in range(5):
        above = jnp.zeros_like(total)
        for k in range(15, -1, -1):
            value = out[n, k]
            breakable = jnp.where(brk_rows <= k, value, 0.0)
            out[n, k] = value - breakable * shorter[k] + above * share[k]
            above = above + breakable


STEPS = (
    ((0, 256), (256, 256), (512, 256)),
    ((768, 192), (960, 192)),
    ((1152, 144),),
)


def kernel(
    decay, floe_hbm, courant_hbm, spectra_hbm, picks_hbm, slot_hbm, weight_hbm, thick_hbm, edge_hbm,
    strain_hbm, ice_hbm, brk_hbm, out,
    floe, courant, spectra, picks, slot, weight, thick, edge, strain, ice, brk,
    choose, x0, x1, x2, r0, r1, r2, tail_send, tail_mid, tail_pass, tail_recv,
    row_send, row_recv, col_send, col_recv, side,
    table, mixing, decay_table, paths, att, hist,
    load_sem, send_sem, recv_sem, own_sem, halo_send, halo_recv, group_sem
):
    x, zc, s = coords()
    me = (x * 16 + zc) * 4 + s
    me_slot = (zc * 4 + x) * 4 + s
    barrier = pltpu.get_barrier_semaphore()
    for i in range(1, 16):
        pl.semaphore_signal(barrier, inc=1, device_id=zc_peer(i, x, zc, s), device_id_type=MESH)
        pl.semaphore_signal(barrier, inc=1, device_id=xy_peer(i, x, zc, s), device_id_type=MESH)
    pairs = (
        (picks_hbm, picks), (spectra_hbm, spectra), (floe_hbm, floe), (courant_hbm, courant),
        (slot_hbm, slot), (weight_hbm, weight), (thick_hbm, thick), (edge_hbm, edge),
        (strain_hbm, strain), (ice_hbm, ice), (brk_hbm, brk),
    )
    loads = [
        pltpu.make_async_copy(src, dst, load_sem.at[k]) for k, (src, dst) in enumerate(pairs)
    ]
    for copy in loads:
        copy.start()
    loads[0].wait()
    choose_cells(picks, choose)
    pl.semaphore_wait(barrier, 30)
    for i in range(1, 16):
        pl.semaphore_signal(group_sem, inc=1, device_id=xy_peer(i, x, zc, s), device_id_type=MESH)
    loads[1].wait()
    sends, lands = (x0, x1, x2), (r0, r1, r2)
    senders = [
        sender(sends[k], lands[k], send_sem.at[k], recv_sem.at[k]) for k in range(3)
    ]
    gather_rows(choose, spectra, *RANGES[0], x0)
    senders[0][0]()
    gather_rows(choose, spectra, *RANGES[1], x1)
    gather_rows(choose, spectra, *RANGES[2], x2)
    gather_tail(choose, spectra, tail_send)
    for copy in loads[2:]:
        copy.wait()
    pack_halo(floe, courant, row_send, col_send)
    pl.semaphore_wait(group_sem, 15)

    def zc_number(device):
        return lax.rem(device[0], 16)

    def xy_number(device):
        return device[0] // 16 * 4 + device[1]

    halo = halo_copies(row_send, row_recv, col_send, col_recv, halo_send, halo_recv)
    for copy in halo:
        copy.start()
    own = [
        pltpu.make_async_copy(sends[k].at[me], lands[k].at[me_slot], own_sem.at[k])
        for k in range(3)
    ]
    own.append(pltpu.make_async_copy(tail_send.at[zc], tail_mid.at[zc], own_sem.at[3]))
    for copy in own:
        copy.start()
    send_group(zc_peer, zc_number, tail_send, tail_mid, zc, send_sem.at[3], recv_sem.at[3])
    senders[0][1]()
    senders[1][0]()
    senders[1][1]()

    fifteen = pl.ds(0, 15)
    own[3].wait()
    pltpu.make_async_copy(tail_send.at[fifteen], tail_mid.at[fifteen], recv_sem.at[3]).wait()
    regroup_tail(tail_mid, tail_pass)
    own_tail = pltpu.make_async_copy(
        tail_pass.at[x * 4 + s], tail_recv.at[x * 4 + s], own_sem.at[4]
    )
    own_tail.start()
    send_group(xy_peer, xy_number, tail_pass, tail_recv, x * 4 + s, send_sem.at[4], recv_sem.at[4])

    fill_decay(decay, decay_table)
    fill_paths(thick, edge, paths)

    def mix_row(r, carry):
        build_mixing(r, slot, weight, mixing)
        return carry

    lax.fori_loop(0, 8, mix_row, 0)
    for copy in halo:
        copy.wait()
    unpack_columns(col_recv, side)
    transport(floe, courant, row_recv, side, out)

    senders[2][0]()
    senders[2][1]()
    own_tail.wait()
    pltpu.make_async_copy(tail_pass.at[fifteen], tail_recv.at[fifteen], recv_sem.at[4]).wait()
    finish_tail(tail_recv, table)

    others = pl.ds(0, N_DEV - 1)
    for k, (first, size) in enumerate(RANGES):
        own[k].wait()
        pltpu.make_async_copy(sends[k].at[others], lands[k].at[others], recv_sem.at[k]).wait()
        transpose_in(lands[k], table, first, size)
        bins = slice(STEPS[k][0][0], sum(STEPS[k][-1]))

        def one_row(r, carry):
            attenuate(r, STEPS[k], table, mixing, decay_table, paths, att)
            part = jnp.dot(strain[:, bins], att[bins], preferred_element_type=F32)[:, None, :]
            here = pl.ds(r, 1)
            hist[:, here, :] = part if k == 0 else hist[:, here, :] + part
            return carry

        lax.fori_loop(0, 8, one_row, 0)
    fracture(hist, weight, ice, brk, out)
    for k in range(3):
        pltpu.make_async_copy(sends[k].at[others], lands[k].at[others], send_sem.at[k]).wait()
    pltpu.make_async_copy(tail_send.at[fifteen], tail_mid.at[fifteen], send_sem.at[3]).wait()
    pltpu.make_async_copy(tail_pass.at[fifteen], tail_recv.at[fifteen], send_sem.at[4]).wait()


def shards(
    floe_area, courant, spectra, send_rows, src_slot, src_weight, thickness, edge_angle,
    decay_rate, strain_table, ice_mask, break_bin
):
    operands = (
        floe_area, courant, spectra[0, 0].T, jnp.transpose(send_rows[0, 0], (1, 2, 0)), src_slot,
        src_weight, thickness, edge_angle, strain_table, ice_mask, break_bin
    )
    vmem = pl.BlockSpec(memory_space=pltpu.VMEM)
    return pl.pallas_call(
        kernel,
        out_shape=jax.ShapeDtypeStruct(floe_area.shape, F32),
        in_specs=[pl.BlockSpec(memory_space=pltpu.SMEM)]
        + [pl.BlockSpec(memory_space=pl.ANY)] * len(operands),
        out_specs=vmem,
        scratch_shapes=[pltpu.VMEM(v.shape, v.dtype) for v in operands]
        + [
            pltpu.VMEM((N_DEV * 4, 512), BF16),
            *[pltpu.VMEM((N_DEV, 4, size), BF16) for _, size in RANGES],
            *[pltpu.VMEM((N_DEV, 4, size), BF16) for _, size in RANGES],
            pltpu.VMEM((16, 16, 128), BF16),
            pltpu.VMEM((16, 16, 128), BF16),
            pltpu.VMEM((16, 4, 256), BF16),
            pltpu.VMEM((16, 4, 256), BF16),
            pltpu.VMEM((2, 82, 4, 512), F32),
            pltpu.VMEM((2, 82, 4, 512), F32),
            pltpu.VMEM((2, 8, COLUMN_ROWS), F32),
            pltpu.VMEM((2, 3, 8, COLUMN_ROWS), F32),
            pltpu.VMEM((3, COLUMN_ROWS, 128), F32),
            pltpu.VMEM((NBIN, N_DEV * 4), BF16),
            pltpu.VMEM((8, N_DEV * 4, 512), BF16),
            pltpu.VMEM((NBIN, 128), F32),
            pltpu.VMEM((8, 72, 512), F32),
            pltpu.VMEM((NBIN, 512), BF16),
            pltpu.VMEM((16, 8, 512), F32),
            pltpu.SemaphoreType.DMA((len(operands),)),
            pltpu.SemaphoreType.DMA((5,)),
            pltpu.SemaphoreType.DMA((5,)),
            pltpu.SemaphoreType.DMA((5,)),
            pltpu.SemaphoreType.DMA((8,)),
            pltpu.SemaphoreType.DMA((8,)),
            pltpu.SemaphoreType.REGULAR,
        ],
        compiler_params=pltpu.CompilerParams(
            collective_id=0, has_side_effects=True, vmem_limit_bytes=56 << 20
        ),
    )(decay_rate, *operands)


def solution(mesh):
    in_specs = (
        P(None, None, "sub", "tiles"),
        P(None, "sub", "tiles"),
        P("tiles", "sub", None, None),
        P("tiles", "sub", None, None, None),
        P(None, "sub", "tiles"),
        P(None, "sub", "tiles"),
        P("sub", "tiles"),
        P("sub", "tiles"),
        P(),
        P(),
        P("sub", "tiles"),
        P("sub", "tiles"),
    )
    out_specs = P(None, None, "sub", "tiles")
    return jax.shard_map(shards, mesh=mesh, in_specs=in_specs, out_specs=out_specs, check_vma=False)
```

```python
import functools
import math

import jax
import jax.numpy as jnp
from jax import lax
from jax.experimental import pallas as pl
from jax.experimental.pallas import tpu as pltpu
from jax.sharding import PartitionSpec as P

MESH = pl.DeviceIdType.MESH
F32 = jnp.float32
BF16 = jnp.bfloat16
NDIR = 36
NBIN = 1296
NSUB = 3
N_DEV = 256
RANGES = ((0, 768), (768, 384), (1152, 128))
WIDE = 1280
COLUMN_ROWS = 768


def coords():
    t, s = lax.axis_index("tiles"), lax.axis_index("sub")
    return t // 16, lax.rem(t, 16), s


def zc_peer(i, x, zc, s):
    c = lax.rem(lax.rem(zc, 2) + i % 2, 2)
    z = lax.rem(zc // 2 + i // 2, 8)
    return (x * 16 + z * 2 + c, s)


def xy_peer(i, x, zc, s):
    return (lax.rem(x + i // 4, 4) * 16 + zc, lax.rem(s + i % 4, 4))


def zc_numbers(zc):
    return [
        lax.rem(zc // 2 + i // 2, 8) * 2 + lax.rem(lax.rem(zc, 2) + i % 2, 2) for i in range(16)
    ]


def sender(src, dst, send_sem, recv_sem):
    x, zc, s = coords()
    me = (zc * 4 + x) * 4 + s
    numbers = zc_numbers(zc)

    def send(tile, sub):
        pltpu.make_async_remote_copy(
            src_ref=src.at[tile * 4 + sub],
            dst_ref=dst.at[me],
            send_sem=send_sem,
            recv_sem=recv_sem,
            device_id=(tile, sub),
            device_id_type=MESH,
        ).start()

    def near():
        for number in numbers[1:]:
            send(x * 16 + number, s)

        def one(i, carry):
            send(lax.rem(x + i // 4, 4) * 16 + zc, lax.rem(s + lax.rem(i, 4), 4))
            return carry

        lax.fori_loop(1, 16, one, 0)

    def far():
        def one(i, carry):
            first = lax.rem(x + i // 4, 4) * 16
            sub = lax.rem(s + lax.rem(i, 4), 4)
            for number in numbers[1:]:
                send(first + number, sub)
            return carry

        lax.fori_loop(1, 16, one, 0)

    return near, far


def send_group(peer, number, src, dst, me, send_sem, recv_sem):
    x, zc, s = coords()
    for i in range(1, 16):
        device = peer(i, x, zc, s)
        pltpu.make_async_remote_copy(
            src_ref=src.at[number(device)],
            dst_ref=dst.at[me],
            send_sem=send_sem,
            recv_sem=recv_sem,
            device_id=device,
            device_id_type=MESH,
        ).start()


def choose_cells(picks, choose):
    pick = picks[...].reshape(16, 64).astype(F32)
    pick = jnp.concatenate([pick, jnp.zeros((16, 64), F32)], axis=1).T[:64]
    pick = jnp.broadcast_to(pick.reshape(64, 1, 16), (64, 16, 16)).reshape(N_DEV * 4, 16)
    row = lax.broadcasted_iota(jnp.int32, (N_DEV * 4, 16), 0)
    lane = lax.broadcasted_iota(jnp.int32, (N_DEV * 4, 16), 1)
    column = jnp.sum(jnp.where(lane == lax.rem(row, 16), pick, 0.0), axis=1, keepdims=True)
    cell = lax.broadcasted_iota(jnp.int32, (N_DEV * 4, 512), 1)
    choose[...] = jnp.where(cell == column.astype(jnp.int32), 1.0, 0.0).astype(BF16)


OVER_CELLS = (((1,), (1,)), ((), ()))


def gather_rows(choose, spectra, first, size, dst):
    for lane in range(0, size, 256):
        width = min(256, size - lane)
        start = first + lane
        rows = lax.dot_general(
            choose[...], spectra[start : start + width, :], OVER_CELLS, preferred_element_type=F32
        )
        dst[:, :, lane : lane + width] = rows.astype(BF16).reshape(N_DEV, 4, width)


def gather_tail(choose, spectra, tail_send):
    last = lax.dot_general(
        choose[...], spectra[WIDE:, :], OVER_CELLS, preferred_element_type=F32
    )
    filler = jnp.zeros((64, NBIN - WIDE), F32)
    for zc in range(16):
        pieces = [last[(x * 16 + zc) * 16 : (x * 16 + zc) * 16 + 16] for x in range(4)]
        tail_send[zc] = jnp.concatenate(pieces + [filler], axis=0).T.astype(BF16)


def regroup_tail(tail_mid, tail_pass):
    turned = tail_mid[...].reshape(256, 128).T
    tail_pass[...] = turned[:64].reshape(16, 4, 256)


def finish_tail(tail_recv, table):
    turned = tail_recv[...].reshape(64, 256).T
    for zc in range(0, 16, 2):
        both = jnp.concatenate(
            [turned[zc * 16 : zc * 16 + 16], turned[zc * 16 + 16 : zc * 16 + 32]], axis=1
        )
        table[WIDE:, zc * 64 : zc * 64 + 128] = both


def pack_halo(floe, courant, row_send, col_send):
    for n in range(5):
        row_send[0, n * 16 : n * 16 + 16] = floe[n, :, 0:4, :]
        row_send[1, n * 16 : n * 16 + 16] = floe[n, :, 4:8, :]
    row_send[0, 80:82] = courant[:, 0:4, :]
    row_send[1, 80:82] = courant[:, 4:8, :]
    filler = jnp.zeros((COLUMN_ROWS - 656, 128), F32)
    for side, lanes in ((0, slice(0, 128)), (1, slice(384, 512))):
        strip = jnp.concatenate(
            [floe[:, :, :, lanes].reshape(640, 128), courant[:, :, lanes].reshape(16, 128), filler]
        )
        turned = strip.T
        col_send[side] = turned[0:8] if side == 0 else turned[120:128]


def halo_copies(row_send, row_recv, col_send, col_recv, send_sem, recv_sem):
    t, s = lax.axis_index("tiles"), lax.axis_index("sub")
    n_tiles = lax.axis_size("tiles")
    copies = []

    def add(src, dst, device):
        k = len(copies)
        copies.append(
            pltpu.make_async_remote_copy(
                src_ref=src,
                dst_ref=dst,
                send_sem=send_sem.at[k],
                recv_sem=recv_sem.at[k],
                device_id=device,
                device_id_type=MESH,
            )
        )

    for side, step in ((0, n_tiles - 1), (1, 1)):
        for group, shift in ((0, 0), (1, 3), (2, 1)):
            device = (lax.rem(t + step, n_tiles), lax.rem(s + shift, 4))
            add(col_send.at[side], col_recv.at[side, group], device)
    add(row_send.at[0], row_recv.at[0], (t, lax.rem(s + 3, 4)))
    add(row_send.at[1], row_recv.at[1], (t, lax.rem(s + 1, 4)))
    return copies


def unpack_columns(col_recv, side):
    for group in range(3):
        side[group] = jnp.concatenate(
            [col_recv[0, group], jnp.zeros((112, COLUMN_ROWS), F32), col_recv[1, group]], axis=0
        ).T


def transport(floe, courant, row_recv, side, out):
    s = lax.axis_index("sub")
    row = lax.broadcasted_iota(jnp.int32, (8, 128), 0)

    def frame(own, layer):
        start = layer * 8 if isinstance(layer, int) else pl.multiple_of(layer * 8, 8)
        here = pl.ds(start, 8)
        corner = jnp.where(row < 4, side[1, here], side[2, here])
        top = jnp.concatenate([own, side[0, here]], axis=1)
        halo = jnp.concatenate([row_recv[0, layer], row_recv[1, layer]], axis=0)
        return top, jnp.concatenate([halo, corner], axis=1)

    wide_row = lax.broadcasted_iota(jnp.int32, (8, 640), 0)
    after, before = jnp.where(s < 3, 1.0, 0.0), jnp.where(s > 0, 1.0, 0.0)
    inside = jnp.where(wide_row < 4, after, before)
    parts = []
    for k in range(2):
        top, halo = frame(courant[k], 80 + k)
        parts.append(jnp.concatenate([top, halo * inside], axis=0))
    east, west = jnp.maximum(parts[0], 0.0), jnp.maximum(-parts[0], 0.0)
    north, south = jnp.maximum(parts[1], 0.0), jnp.maximum(-parts[1], 0.0)
    keep = 1.0 - east - west - north - south

    def one(layer):
        n, k = layer // 16, lax.rem(layer, 16)
        v = jnp.concatenate(frame(floe[n, k], layer), axis=0)
        for _ in range(NSUB):
            v = (
                v * keep
                + pltpu.roll(v * east, 1, 1)
                + pltpu.roll(v * west, 639, 1)
                + pltpu.roll(v * north, 1, 0)
                + pltpu.roll(v * south, 15, 0)
            )
        out[n, k] = v[0:8, 0:512]

    def pair(i, carry):
        one(2 * i)
        one(2 * i + 1)
        return carry

    lax.fori_loop(0, 40, pair, 0)


def transpose_in(src, table, first, width):
    for lane in range(0, width, 128):
        size = min(128, width - lane)
        block = src[:, :, lane : lane + 128].reshape(N_DEV * 4, 128)
        turned = block.T
        table[first + lane : first + lane + size, :] = turned[:size]


def build_mixing(r, slot, weight, mixing):
    rows = lax.broadcasted_iota(jnp.int32, (N_DEV * 4, 512), 0).astype(jnp.int16)
    total = jnp.zeros((N_DEV * 4, 512), BF16)
    for k in range(4):
        given = slot[k, pl.ds(r, 1), :]
        slots = lax.rem(given // 16, 16) * 64 + given // 256 * 16 + lax.rem(given, 16)
        slots = slots.astype(jnp.int16)
        weights = weight[k, pl.ds(r, 1), :].astype(BF16)
        total = total + jnp.where(rows == slots, weights, jnp.zeros((), BF16))
    mixing[r] = total


def wide(column, lanes=4):
    return jnp.concatenate([column] * lanes, axis=1)


def fill_decay(decay, decay_table):
    row = lax.broadcasted_iota(jnp.int32, (72, 128), 0)
    for g in range(18):
        decay_table[g * 72 : g * 72 + 72, :] = jnp.where(row < 36, decay[2 * g], decay[2 * g + 1])


def fill_paths(thick, edge, paths):
    direction = lax.rem(lax.broadcasted_iota(jnp.int32, (72, 128), 0), NDIR).astype(F32)
    angle = 2.0 * math.pi * direction / NDIR - math.pi
    trig = (jnp.cos(angle), jnp.sin(angle))
    cos_edge, sin_edge = jnp.cos(edge[...]), jnp.sin(edge[...])
    scaled = -math.log2(math.e) * thick[...]
    for r in range(8):
        cosine = wide(trig[0]) * cos_edge[r : r + 1] + wide(trig[1]) * sin_edge[r : r + 1]
        paths[r] = scaled[r : r + 1] / (0.25 + 0.75 * cosine * cosine)


def attenuate(r, steps, table, mixing, decay_table, paths, att):
    path = paths[r]
    for start, size in steps:
        spectrum = jnp.dot(table[start : start + size, :], mixing[r], preferred_element_type=F32)
        decay_rows = wide(decay_table[start : start + size, :])
        first = start % 72
        pieces, have = [path[first:]], 72 - first
        while have < size:
            pieces.append(path)
            have += 72
        factor = jnp.concatenate(pieces, axis=0)[:size]
        att[start : start + size, :] = (spectrum * jnp.exp2(decay_rows * factor)).astype(BF16)


def fracture(hist, weight, ice, brk, out, out_hbm, out_sem):
    total_w = weight[0] + weight[1] + weight[2] + weight[3]
    used_w = sum(weight[k].astype(BF16).astype(F32) for k in range(4))
    fix = total_w / used_w
    rows = [hist[j] * fix for j in range(16)]
    total = functools.reduce(jnp.add, rows)
    strength = ice[...].astype(F32) * total / (total + 0.005 * 16 * NBIN)
    scale = strength / total
    share = [v * scale for v in rows]
    shorter, run = [], jnp.zeros_like(total)
    for j in range(16):
        shorter.append(run)
        run = run + share[j]
    brk_rows = brk[...]
    for n in range(5):
        above = jnp.zeros_like(total)
        for k in range(15, -1, -1):
            value = out[n, k]
            breakable = jnp.where(brk_rows <= k, value, 0.0)
            out[n, k] = value - breakable * shorter[k] + above * share[k]
            above = above + breakable
        pltpu.make_async_copy(out.at[n], out_hbm.at[n], out_sem.at[n]).start()


STEPS = (
    ((0, 256), (256, 256), (512, 256)),
    ((768, 192), (960, 192)),
    ((1152, 144),),
)
UNROLL = (2, 2, 4)


def kernel(
    decay_hbm, floe_hbm, courant_hbm, spectra_hbm, picks_hbm, slot_hbm, weight_hbm, thick_hbm, edge_hbm,
    strain_hbm, ice_hbm, brk_hbm, out_hbm,
    decay, floe, courant, spectra, picks, slot, weight, thick, edge, strain, ice, brk, out,
    choose, x0, x1, x2, r0, r1, r2, tail_send, tail_mid, tail_pass, tail_recv,
    row_send, row_recv, col_send, col_recv, side,
    table, mixing, decay_table, paths, att, hist,
    load_sem, send_sem, recv_sem, own_sem, halo_send, halo_recv, out_sem, group_sem
):
    x, zc, s = coords()
    me = (x * 16 + zc) * 4 + s
    me_slot = (zc * 4 + x) * 4 + s
    barrier = pltpu.get_barrier_semaphore()
    for i in range(1, 16):
        pl.semaphore_signal(barrier, inc=1, device_id=zc_peer(i, x, zc, s), device_id_type=MESH)
        pl.semaphore_signal(barrier, inc=1, device_id=xy_peer(i, x, zc, s), device_id_type=MESH)
    pairs = (
        (picks_hbm, picks), (spectra_hbm, spectra), (floe_hbm, floe), (courant_hbm, courant),
        (slot_hbm, slot), (weight_hbm, weight), (thick_hbm, thick), (edge_hbm, edge),
        (strain_hbm, strain), (ice_hbm, ice), (brk_hbm, brk), (decay_hbm, decay),
    )
    loads = [
        pltpu.make_async_copy(src, dst, load_sem.at[k]) for k, (src, dst) in enumerate(pairs)
    ]
    for copy in loads:
        copy.start()
    loads[0].wait()
    choose_cells(picks, choose)
    pl.semaphore_wait(barrier, 30)
    for i in range(1, 16):
        pl.semaphore_signal(group_sem, inc=1, device_id=xy_peer(i, x, zc, s), device_id_type=MESH)
    loads[1].wait()
    sends, lands = (x0, x1, x2), (r0, r1, r2)
    senders = [
        sender(sends[k], lands[k], send_sem.at[k], recv_sem.at[k]) for k in range(3)
    ]
    gather_rows(choose, spectra, *RANGES[0], x0)
    senders[0][0]()
    gather_tail(choose, spectra, tail_send)
    for copy in loads[2:]:
        copy.wait()
    pack_halo(floe, courant, row_send, col_send)
    pl.semaphore_wait(group_sem, 15)

    def zc_number(device):
        return lax.rem(device[0], 16)

    def xy_number(device):
        return device[0] // 16 * 4 + device[1]

    halo = halo_copies(row_send, row_recv, col_send, col_recv, halo_send, halo_recv)
    for copy in halo:
        copy.start()
    own = [
        pltpu.make_async_copy(sends[k].at[me], lands[k].at[me_slot], own_sem.at[k])
        for k in range(3)
    ]
    own.append(pltpu.make_async_copy(tail_send.at[zc], tail_mid.at[zc], own_sem.at[3]))
    own[3].start()
    send_group(zc_peer, zc_number, tail_send, tail_mid, zc, send_sem.at[3], recv_sem.at[3])
    senders[0][1]()
    own[0].start()

    fifteen = pl.ds(0, 15)
    own[3].wait()
    pltpu.make_async_copy(tail_send.at[fifteen], tail_mid.at[fifteen], recv_sem.at[3]).wait()
    regroup_tail(tail_mid, tail_pass)
    own_tail = pltpu.make_async_copy(
        tail_pass.at[x * 4 + s], tail_recv.at[x * 4 + s], own_sem.at[4]
    )
    own_tail.start()
    send_group(xy_peer, xy_number, tail_pass, tail_recv, x * 4 + s, send_sem.at[4], recv_sem.at[4])
    for k in (1, 2):
        gather_rows(choose, spectra, *RANGES[k], sends[k])
        own[k].start()
    senders[1][0]()
    senders[1][1]()

    fill_decay(decay, decay_table)
    fill_paths(thick, edge, paths)

    def mix_row(r, carry):
        build_mixing(r, slot, weight, mixing)
        return carry

    lax.fori_loop(0, 8, mix_row, 0)
    for copy in halo:
        copy.wait()
    unpack_columns(col_recv, side)
    transport(floe, courant, row_recv, side, out)

    senders[2][0]()
    senders[2][1]()
    others = pl.ds(0, N_DEV - 1)
    for k, (first, size) in enumerate(RANGES):
        if k == 2:
            own_tail.wait()
            pltpu.make_async_copy(
                tail_pass.at[fifteen], tail_recv.at[fifteen], recv_sem.at[4]
            ).wait()
            finish_tail(tail_recv, table)
        own[k].wait()
        pltpu.make_async_copy(sends[k].at[others], lands[k].at[others], recv_sem.at[k]).wait()
        transpose_in(lands[k], table, first, size)
        bins = slice(STEPS[k][0][0], sum(STEPS[k][-1]))

        def some_rows(i, carry):
            for u in range(UNROLL[k]):
                r = i * UNROLL[k] + u
                attenuate(r, STEPS[k], table, mixing, decay_table, paths, att.at[u])
                part = jnp.dot(strain[:, bins], att[u, bins], preferred_element_type=F32)
                here = pl.ds(r, 1)
                hist[:, here, :] = part[:, None] if k == 0 else hist[:, here, :] + part[:, None]
            return carry

        lax.fori_loop(0, 8 // UNROLL[k], some_rows, 0)
    fracture(hist, weight, ice, brk, out, out_hbm, out_sem)
    for k in range(3):
        pltpu.make_async_copy(sends[k].at[others], lands[k].at[others], send_sem.at[k]).wait()
    pltpu.make_async_copy(tail_send.at[fifteen], tail_mid.at[fifteen], send_sem.at[3]).wait()
    pltpu.make_async_copy(tail_pass.at[fifteen], tail_recv.at[fifteen], send_sem.at[4]).wait()
    for n in range(5):
        pltpu.make_async_copy(out.at[n], out_hbm.at[n], out_sem.at[n]).wait()


def shards(
    floe_area, courant, spectra, send_rows, src_slot, src_weight, thickness, edge_angle,
    decay_rate, strain_table, ice_mask, break_bin
):
    operands = (
        floe_area, courant, spectra[0, 0].T, jnp.transpose(send_rows[0, 0], (1, 2, 0)), src_slot,
        src_weight, thickness, edge_angle, strain_table, ice_mask, break_bin
    )
    anywhere = pl.BlockSpec(memory_space=pl.ANY)
    return pl.pallas_call(
        kernel,
        out_shape=jax.ShapeDtypeStruct(floe_area.shape, F32),
        in_specs=[anywhere] * (len(operands) + 1),
        out_specs=anywhere,
        scratch_shapes=[pltpu.SMEM(decay_rate.shape, F32)]
        + [pltpu.VMEM(v.shape, v.dtype) for v in (*operands, floe_area)]
        + [
            pltpu.VMEM((N_DEV * 4, 512), BF16),
            *[pltpu.VMEM((N_DEV, 4, size), BF16) for _, size in RANGES],
            *[pltpu.VMEM((N_DEV, 4, size), BF16) for _, size in RANGES],
            pltpu.VMEM((16, 16, 128), BF16),
            pltpu.VMEM((16, 16, 128), BF16),
            pltpu.VMEM((16, 4, 256), BF16),
            pltpu.VMEM((16, 4, 256), BF16),
            pltpu.VMEM((2, 82, 4, 512), F32),
            pltpu.VMEM((2, 82, 4, 512), F32),
            pltpu.VMEM((2, 8, COLUMN_ROWS), F32),
            pltpu.VMEM((2, 3, 8, COLUMN_ROWS), F32),
            pltpu.VMEM((3, COLUMN_ROWS, 128), F32),
            pltpu.VMEM((NBIN, N_DEV * 4), BF16),
            pltpu.VMEM((8, N_DEV * 4, 512), BF16),
            pltpu.VMEM((NBIN, 128), F32),
            pltpu.VMEM((8, 72, 512), F32),
            pltpu.VMEM((4, NBIN, 512), BF16),
            pltpu.VMEM((16, 8, 512), F32),
            pltpu.SemaphoreType.DMA((len(operands) + 1,)),
            pltpu.SemaphoreType.DMA((5,)),
            pltpu.SemaphoreType.DMA((5,)),
            pltpu.SemaphoreType.DMA((5,)),
            pltpu.SemaphoreType.DMA((8,)),
            pltpu.SemaphoreType.DMA((8,)),
            pltpu.SemaphoreType.DMA((5,)),
            pltpu.SemaphoreType.REGULAR,
        ],
        compiler_params=pltpu.CompilerParams(
            collective_id=0, has_side_effects=True, vmem_limit_bytes=56 << 20
        ),
    )(decay_rate, *operands)


def solution(mesh):
    in_specs = (
        P(None, None, "sub", "tiles"),
        P(None, "sub", "tiles"),
        P("tiles", "sub", None, None),
        P("tiles", "sub", None, None, None),
        P(None, "sub", "tiles"),
        P(None, "sub", "tiles"),
        P("sub", "tiles"),
        P("sub", "tiles"),
        P(),
        P(),
        P("sub", "tiles"),
        P("sub", "tiles"),
    )
    out_specs = P(None, None, "sub", "tiles")
    return jax.shard_map(shards, mesh=mesh, in_specs=in_specs, out_specs=out_specs, check_vma=False)
```

```python
import functools
import math

import jax
import jax.numpy as jnp
from jax import lax
from jax.experimental import pallas as pl
from jax.experimental.pallas import tpu as pltpu
from jax.sharding import PartitionSpec as P

MESH = pl.DeviceIdType.MESH
F32 = jnp.float32
BF16 = jnp.bfloat16
NDIR = 36
NBIN = 1296
NSUB = 3
N_DEV = 256
RANGES = ((0, 768), (768, 384), (1152, 128))
WIDE = 1280
COLUMN_ROWS = 768


def coords():
    t, s = lax.axis_index("tiles"), lax.axis_index("sub")
    return t // 16, lax.rem(t, 16), s


def zc_peer(i, x, zc, s):
    c = lax.rem(lax.rem(zc, 2) + i % 2, 2)
    z = lax.rem(zc // 2 + i // 2, 8)
    return (x * 16 + z * 2 + c, s)


def xy_peer(i, x, zc, s):
    return (lax.rem(x + i // 4, 4) * 16 + zc, lax.rem(s + i % 4, 4))


def zc_numbers(zc):
    return [
        lax.rem(zc // 2 + i // 2, 8) * 2 + lax.rem(lax.rem(zc, 2) + i % 2, 2) for i in range(16)
    ]


def sender(src, dst, send_sem, recv_sem):
    x, zc, s = coords()
    me = (zc * 4 + x) * 4 + s
    numbers = zc_numbers(zc)

    def send(tile, sub):
        pltpu.make_async_remote_copy(
            src_ref=src.at[tile * 4 + sub],
            dst_ref=dst.at[me],
            send_sem=send_sem,
            recv_sem=recv_sem,
            device_id=(tile, sub),
            device_id_type=MESH,
        ).start()

    def near():
        for number in numbers[1:]:
            send(x * 16 + number, s)

        def one(i, carry):
            send(lax.rem(x + i // 4, 4) * 16 + zc, lax.rem(s + lax.rem(i, 4), 4))
            return carry

        lax.fori_loop(1, 16, one, 0)

    def far():
        def one(i, carry):
            first = lax.rem(x + i // 4, 4) * 16
            sub = lax.rem(s + lax.rem(i, 4), 4)
            for number in numbers[1:]:
                send(first + number, sub)
            return carry

        lax.fori_loop(1, 16, one, 0)

    return near, far


def send_group(peer, number, src, dst, me, send_sem, recv_sem):
    x, zc, s = coords()
    for i in range(1, 16):
        device = peer(i, x, zc, s)
        pltpu.make_async_remote_copy(
            src_ref=src.at[number(device)],
            dst_ref=dst.at[me],
            send_sem=send_sem,
            recv_sem=recv_sem,
            device_id=device,
            device_id_type=MESH,
        ).start()


def choose_cells(picks, choose):
    pick = picks[...].reshape(16, 64).astype(F32)
    pick = jnp.concatenate([pick, jnp.zeros((16, 64), F32)], axis=1).T[:64]
    pick = jnp.broadcast_to(pick.reshape(64, 1, 16), (64, 16, 16)).reshape(N_DEV * 4, 16)
    row = lax.broadcasted_iota(jnp.int32, (N_DEV * 4, 16), 0)
    lane = lax.broadcasted_iota(jnp.int32, (N_DEV * 4, 16), 1)
    column = jnp.sum(jnp.where(lane == lax.rem(row, 16), pick, 0.0), axis=1, keepdims=True)
    cell = lax.broadcasted_iota(jnp.int32, (N_DEV * 4, 512), 1)
    choose[...] = jnp.where(cell == column.astype(jnp.int32), 1.0, 0.0).astype(BF16)


OVER_CELLS = (((1,), (1,)), ((), ()))


def gather_rows(choose, spectra, first, size, dst):
    for lane in range(0, size, 256):
        width = min(256, size - lane)
        start = first + lane
        rows = lax.dot_general(
            choose[...], spectra[start : start + width, :], OVER_CELLS, preferred_element_type=F32
        )
        dst[:, :, lane : lane + width] = rows.astype(BF16).reshape(N_DEV, 4, width)


def gather_tail(choose, spectra, tail_send):
    last = lax.dot_general(
        choose[...], spectra[WIDE:, :], OVER_CELLS, preferred_element_type=F32
    )
    filler = jnp.zeros((64, NBIN - WIDE), F32)
    for zc in range(16):
        pieces = [last[(x * 16 + zc) * 16 : (x * 16 + zc) * 16 + 16] for x in range(4)]
        tail_send[zc] = jnp.concatenate(pieces + [filler], axis=0).T.astype(BF16)


def regroup_tail(tail_mid, tail_pass):
    turned = tail_mid[...].reshape(256, 128).T
    tail_pass[...] = turned[:64].reshape(16, 4, 256)


def finish_tail(tail_recv, table):
    turned = tail_recv[...].reshape(64, 256).T
    for zc in range(0, 16, 2):
        both = jnp.concatenate(
            [turned[zc * 16 : zc * 16 + 16], turned[zc * 16 + 16 : zc * 16 + 32]], axis=1
        )
        table[WIDE:, zc * 64 : zc * 64 + 128] = both


def pack_halo(floe, courant, row_send, col_send):
    for n in range(5):
        row_send[0, n * 16 : n * 16 + 16] = floe[n, :, 0:4, :]
        row_send[1, n * 16 : n * 16 + 16] = floe[n, :, 4:8, :]
    row_send[0, 80:82] = courant[:, 0:4, :]
    row_send[1, 80:82] = courant[:, 4:8, :]
    filler = jnp.zeros((COLUMN_ROWS - 656, 128), F32)
    for side, lanes in ((0, slice(0, 128)), (1, slice(384, 512))):
        strip = jnp.concatenate(
            [floe[:, :, :, lanes].reshape(640, 128), courant[:, :, lanes].reshape(16, 128), filler]
        )
        turned = strip.T
        col_send[side] = turned[0:8] if side == 0 else turned[120:128]


def halo_copies(row_send, row_recv, col_send, col_recv, send_sem, recv_sem):
    t, s = lax.axis_index("tiles"), lax.axis_index("sub")
    n_tiles = lax.axis_size("tiles")
    copies = []

    def add(src, dst, device):
        k = len(copies)
        copies.append(
            pltpu.make_async_remote_copy(
                src_ref=src,
                dst_ref=dst,
                send_sem=send_sem.at[k],
                recv_sem=recv_sem.at[k],
                device_id=device,
                device_id_type=MESH,
            )
        )

    for side, step in ((0, n_tiles - 1), (1, 1)):
        for group, shift in ((0, 0), (1, 3), (2, 1)):
            device = (lax.rem(t + step, n_tiles), lax.rem(s + shift, 4))
            add(col_send.at[side], col_recv.at[side, group], device)
    add(row_send.at[0], row_recv.at[0], (t, lax.rem(s + 3, 4)))
    add(row_send.at[1], row_recv.at[1], (t, lax.rem(s + 1, 4)))
    return copies


def unpack_columns(col_recv, side):
    for group in range(3):
        side[group] = jnp.concatenate(
            [col_recv[0, group], jnp.zeros((112, COLUMN_ROWS), F32), col_recv[1, group]], axis=0
        ).T


def transport(floe, courant, row_recv, side, out):
    s = lax.axis_index("sub")
    row = lax.broadcasted_iota(jnp.int32, (8, 128), 0)

    def frame(own, layer):
        start = layer * 8 if isinstance(layer, int) else pl.multiple_of(layer * 8, 8)
        here = pl.ds(start, 8)
        corner = jnp.where(row < 4, side[1, here], side[2, here])
        top = jnp.concatenate([own, side[0, here]], axis=1)
        halo = jnp.concatenate([row_recv[0, layer], row_recv[1, layer]], axis=0)
        return top, jnp.concatenate([halo, corner], axis=1)

    wide_row = lax.broadcasted_iota(jnp.int32, (8, 640), 0)
    after, before = jnp.where(s < 3, 1.0, 0.0), jnp.where(s > 0, 1.0, 0.0)
    inside = jnp.where(wide_row < 4, after, before)
    parts = []
    for k in range(2):
        top, halo = frame(courant[k], 80 + k)
        parts.append(jnp.concatenate([top, halo * inside], axis=0))
    east, west = jnp.maximum(parts[0], 0.0), jnp.maximum(-parts[0], 0.0)
    north, south = jnp.maximum(parts[1], 0.0), jnp.maximum(-parts[1], 0.0)
    keep = 1.0 - east - west - north - south

    def one(layer):
        n, k = layer // 16, lax.rem(layer, 16)
        v = jnp.concatenate(frame(floe[n, k], layer), axis=0)
        for _ in range(NSUB):
            v = (
                v * keep
                + pltpu.roll(v * east, 1, 1)
                + pltpu.roll(v * west, 639, 1)
                + pltpu.roll(v * north, 1, 0)
                + pltpu.roll(v * south, 15, 0)
            )
        out[n, k] = v[0:8, 0:512]

    def pair(i, carry):
        one(2 * i)
        one(2 * i + 1)
        return carry

    lax.fori_loop(0, 40, pair, 0)


def transpose_in(src, table, first, width):
    for lane in range(0, width, 128):
        size = min(128, width - lane)
        block = src[:, :, lane : lane + 128].reshape(N_DEV * 4, 128)
        turned = block.T
        table[first + lane : first + lane + size, :] = turned[:size]


def build_mixing(r, slot, weight, mixing):
    rows = lax.broadcasted_iota(jnp.int32, (N_DEV * 4, 512), 0).astype(jnp.int16)
    total = jnp.zeros((N_DEV * 4, 512), BF16)
    for k in range(4):
        given = slot[k, pl.ds(r, 1), :]
        slots = lax.rem(given // 16, 16) * 64 + given // 256 * 16 + lax.rem(given, 16)
        slots = slots.astype(jnp.int16)
        weights = weight[k, pl.ds(r, 1), :].astype(BF16)
        total = total + jnp.where(rows == slots, weights, jnp.zeros((), BF16))
    mixing[r] = total


def wide(column, lanes=4):
    return jnp.concatenate([column] * lanes, axis=1)


def fill_decay(decay, decay_table):
    row = lax.broadcasted_iota(jnp.int32, (72, 128), 0)
    for g in range(18):
        decay_table[g * 72 : g * 72 + 72, :] = jnp.where(row < 36, decay[2 * g], decay[2 * g + 1])


def fill_paths(thick, edge, paths):
    direction = lax.rem(lax.broadcasted_iota(jnp.int32, (72, 128), 0), NDIR).astype(F32)
    angle = 2.0 * math.pi * direction / NDIR - math.pi
    trig = (jnp.cos(angle), jnp.sin(angle))
    cos_edge, sin_edge = jnp.cos(edge[...]), jnp.sin(edge[...])
    scaled = -math.log2(math.e) * thick[...]
    for r in range(8):
        cosine = wide(trig[0]) * cos_edge[r : r + 1] + wide(trig[1]) * sin_edge[r : r + 1]
        paths[r] = scaled[r : r + 1] / (0.25 + 0.75 * cosine * cosine)


def damping(r, start, size, decay_table, paths):
    path = paths[r]
    first = start % 72
    pieces, have = [path[first:]], 72 - first
    while have < size:
        pieces.append(path)
        have += 72
    factor = jnp.concatenate(pieces, axis=0)[:size]
    return jnp.exp2(wide(decay_table[start : start + size, :]) * factor)


def attenuate(r, steps, table, mixing, damp, att):
    for start, size in steps:
        spectrum = jnp.dot(table[start : start + size, :], mixing[r], preferred_element_type=F32)
        att[start : start + size, :] = (spectrum * damp(r, start, size)).astype(BF16)


def fracture(hist, weight, ice, brk, out):
    total_w = weight[0] + weight[1] + weight[2] + weight[3]
    used_w = sum(weight[k].astype(BF16).astype(F32) for k in range(4))
    fix = total_w / used_w
    rows = [hist[j] * fix for j in range(16)]
    total = functools.reduce(jnp.add, rows)
    strength = ice[...].astype(F32) * total / (total + 0.005 * 16 * NBIN)
    scale = strength / total
    share = [v * scale for v in rows]
    shorter, run = [], jnp.zeros_like(total)
    for j in range(16):
        shorter.append(run)
        run = run + share[j]
    brk_rows = brk[...]
    for n in range(5):
        above = jnp.zeros_like(total)
        for k in range(15, -1, -1):
            value = out[n, k]
            breakable = jnp.where(brk_rows <= k, value, 0.0)
            out[n, k] = value - breakable * shorter[k] + above * share[k]
            above = above + breakable


STEPS = (
    ((0, 256), (256, 256), (512, 256)),
    ((768, 192), (960, 192)),
    ((1152, 144),),
)
UNROLL = (2, 2, 4)


def kernel(
    decay_hbm, floe_hbm, courant_hbm, spectra_hbm, picks_hbm, slot_hbm, weight_hbm, thick_hbm, edge_hbm,
    strain_hbm, ice_hbm, brk_hbm, out,
    decay, floe, courant, spectra, picks, slot, weight, thick, edge, strain, ice, brk,
    choose, x0, x1, x2, r0, r1, r2, tail_send, tail_mid, tail_pass, tail_recv,
    row_send, row_recv, col_send, col_recv, side,
    table, mixing, decay_table, paths, last_damping, att, hist,
    load_sem, send_sem, recv_sem, own_sem, halo_send, halo_recv, group_sem
):
    x, zc, s = coords()
    me = (x * 16 + zc) * 4 + s
    me_slot = (zc * 4 + x) * 4 + s
    barrier = pltpu.get_barrier_semaphore()
    for i in range(1, 16):
        pl.semaphore_signal(barrier, inc=1, device_id=zc_peer(i, x, zc, s), device_id_type=MESH)
        pl.semaphore_signal(barrier, inc=1, device_id=xy_peer(i, x, zc, s), device_id_type=MESH)
    pairs = (
        (picks_hbm, picks), (spectra_hbm, spectra), (floe_hbm, floe), (courant_hbm, courant),
        (slot_hbm, slot), (weight_hbm, weight), (thick_hbm, thick), (edge_hbm, edge),
        (strain_hbm, strain), (ice_hbm, ice), (brk_hbm, brk), (decay_hbm, decay),
    )
    loads = [
        pltpu.make_async_copy(src, dst, load_sem.at[k]) for k, (src, dst) in enumerate(pairs)
    ]
    for copy in loads:
        copy.start()
    loads[0].wait()
    choose_cells(picks, choose)
    pl.semaphore_wait(barrier, 30)
    for i in range(1, 16):
        pl.semaphore_signal(group_sem, inc=1, device_id=xy_peer(i, x, zc, s), device_id_type=MESH)
    loads[1].wait()
    sends, lands = (x0, x1, x2), (r0, r1, r2)
    senders = [
        sender(sends[k], lands[k], send_sem.at[k], recv_sem.at[k]) for k in range(3)
    ]
    gather_rows(choose, spectra, *RANGES[0], x0)
    senders[0][0]()
    gather_tail(choose, spectra, tail_send)
    for copy in loads[2:]:
        copy.wait()
    pack_halo(floe, courant, row_send, col_send)
    pl.semaphore_wait(group_sem, 15)

    def zc_number(device):
        return lax.rem(device[0], 16)

    def xy_number(device):
        return device[0] // 16 * 4 + device[1]

    halo = halo_copies(row_send, row_recv, col_send, col_recv, halo_send, halo_recv)
    for copy in halo:
        copy.start()
    own = [
        pltpu.make_async_copy(sends[k].at[me], lands[k].at[me_slot], own_sem.at[k])
        for k in range(3)
    ]
    own.append(pltpu.make_async_copy(tail_send.at[zc], tail_mid.at[zc], own_sem.at[3]))
    own[3].start()
    send_group(zc_peer, zc_number, tail_send, tail_mid, zc, send_sem.at[3], recv_sem.at[3])
    senders[0][1]()
    own[0].start()

    fifteen = pl.ds(0, 15)
    own[3].wait()
    pltpu.make_async_copy(tail_send.at[fifteen], tail_mid.at[fifteen], recv_sem.at[3]).wait()
    regroup_tail(tail_mid, tail_pass)
    own_tail = pltpu.make_async_copy(
        tail_pass.at[x * 4 + s], tail_recv.at[x * 4 + s], own_sem.at[4]
    )
    own_tail.start()
    send_group(xy_peer, xy_number, tail_pass, tail_recv, x * 4 + s, send_sem.at[4], recv_sem.at[4])
    for k in (1, 2):
        gather_rows(choose, spectra, *RANGES[k], sends[k])
        own[k].start()
    senders[1][0]()
    senders[1][1]()

    fill_decay(decay, decay_table)
    fill_paths(thick, edge, paths)

    def mix_row(r, carry):
        build_mixing(r, slot, weight, mixing)
        last_damping[r] = damping(r, *STEPS[2][0], decay_table, paths)
        return carry

    lax.fori_loop(0, 8, mix_row, 0)
    for copy in halo:
        copy.wait()
    unpack_columns(col_recv, side)
    transport(floe, courant, row_recv, side, out)

    senders[2][0]()
    senders[2][1]()
    def damp(r, start, size):
        if (start, size) == STEPS[2][0]:
            return last_damping[r]
        return damping(r, start, size, decay_table, paths)

    others = pl.ds(0, N_DEV - 1)
    for k, (first, size) in enumerate(RANGES):
        if k == 2:
            own_tail.wait()
            pltpu.make_async_copy(
                tail_pass.at[fifteen], tail_recv.at[fifteen], recv_sem.at[4]
            ).wait()
            finish_tail(tail_recv, table)
        own[k].wait()
        pltpu.make_async_copy(sends[k].at[others], lands[k].at[others], recv_sem.at[k]).wait()
        transpose_in(lands[k], table, first, size)
        bins = slice(STEPS[k][0][0], sum(STEPS[k][-1]))

        def some_rows(i, carry):
            for u in range(UNROLL[k]):
                r = i * UNROLL[k] + u
                attenuate(r, STEPS[k], table, mixing, damp, att.at[u])
                part = jnp.dot(strain[:, bins], att[u, bins], preferred_element_type=F32)
                here = pl.ds(r, 1)
                hist[:, here, :] = part[:, None] if k == 0 else hist[:, here, :] + part[:, None]
            return carry

        lax.fori_loop(0, 8 // UNROLL[k], some_rows, 0)
    fracture(hist, weight, ice, brk, out)
    for k in range(3):
        pltpu.make_async_copy(sends[k].at[others], lands[k].at[others], send_sem.at[k]).wait()
    pltpu.make_async_copy(tail_send.at[fifteen], tail_mid.at[fifteen], send_sem.at[3]).wait()
    pltpu.make_async_copy(tail_pass.at[fifteen], tail_recv.at[fifteen], send_sem.at[4]).wait()


def shards(
    floe_area, courant, spectra, send_rows, src_slot, src_weight, thickness, edge_angle,
    decay_rate, strain_table, ice_mask, break_bin
):
    operands = (
        floe_area, courant, spectra[0, 0].T, jnp.transpose(send_rows[0, 0], (1, 2, 0)), src_slot,
        src_weight, thickness, edge_angle, strain_table, ice_mask, break_bin
    )
    anywhere = pl.BlockSpec(memory_space=pl.ANY)
    return pl.pallas_call(
        kernel,
        out_shape=pltpu.VMEM(floe_area.shape, F32),
        in_specs=[anywhere] * (len(operands) + 1),
        out_specs=pl.BlockSpec(memory_space=pltpu.VMEM),
        scratch_shapes=[pltpu.SMEM(decay_rate.shape, F32)]
        + [pltpu.VMEM(v.shape, v.dtype) for v in operands]
        + [
            pltpu.VMEM((N_DEV * 4, 512), BF16),
            *[pltpu.VMEM((N_DEV, 4, size), BF16) for _, size in RANGES],
            *[pltpu.VMEM((N_DEV, 4, size), BF16) for _, size in RANGES],
            pltpu.VMEM((16, 16, 128), BF16),
            pltpu.VMEM((16, 16, 128), BF16),
            pltpu.VMEM((16, 4, 256), BF16),
            pltpu.VMEM((16, 4, 256), BF16),
            pltpu.VMEM((2, 82, 4, 512), F32),
            pltpu.VMEM((2, 82, 4, 512), F32),
            pltpu.VMEM((2, 8, COLUMN_ROWS), F32),
            pltpu.VMEM((2, 3, 8, COLUMN_ROWS), F32),
            pltpu.VMEM((3, COLUMN_ROWS, 128), F32),
            pltpu.VMEM((NBIN, N_DEV * 4), BF16),
            pltpu.VMEM((8, N_DEV * 4, 512), BF16),
            pltpu.VMEM((NBIN, 128), F32),
            pltpu.VMEM((8, 72, 512), F32),
            pltpu.VMEM((8, STEPS[2][0][1], 512), F32),
            pltpu.VMEM((4, NBIN, 512), BF16),
            pltpu.VMEM((16, 8, 512), F32),
            pltpu.SemaphoreType.DMA((len(operands) + 1,)),
            pltpu.SemaphoreType.DMA((5,)),
            pltpu.SemaphoreType.DMA((5,)),
            pltpu.SemaphoreType.DMA((5,)),
            pltpu.SemaphoreType.DMA((8,)),
            pltpu.SemaphoreType.DMA((8,)),
            pltpu.SemaphoreType.REGULAR,
        ],
        compiler_params=pltpu.CompilerParams(
            collective_id=0, has_side_effects=True, vmem_limit_bytes=56 << 20
        ),
    )(decay_rate, *operands)


def solution(mesh):
    in_specs = (
        P(None, None, "sub", "tiles"),
        P(None, "sub", "tiles"),
        P("tiles", "sub", None, None),
        P("tiles", "sub", None, None, None),
        P(None, "sub", "tiles"),
        P(None, "sub", "tiles"),
        P("sub", "tiles"),
        P("sub", "tiles"),
        P(),
        P(),
        P("sub", "tiles"),
        P("sub", "tiles"),
    )
    out_specs = P(None, None, "sub", "tiles")
    return jax.shard_map(shards, mesh=mesh, in_specs=in_specs, out_specs=out_specs, check_vma=False)
```

```python
import functools
import math

import jax
import jax.numpy as jnp
from jax import lax
from jax.experimental import pallas as pl
from jax.experimental.pallas import tpu as pltpu
from jax.sharding import PartitionSpec as P

MESH = pl.DeviceIdType.MESH
F32 = jnp.float32
BF16 = jnp.bfloat16
NDIR = 36
NBIN = 1296
NSUB = 3
N_DEV = 256
RANGES = ((0, 896), (896, 256), (1152, 128))
WIDE = 1280
COLUMN_ROWS = 768


def coords():
    t, s = lax.axis_index("tiles"), lax.axis_index("sub")
    return t // 16, lax.rem(t, 16), s


def zc_peer(i, x, zc, s):
    c = lax.rem(lax.rem(zc, 2) + i % 2, 2)
    z = lax.rem(zc // 2 + i // 2, 8)
    return (x * 16 + z * 2 + c, s)


def xy_peer(i, x, zc, s):
    return (lax.rem(x + i // 4, 4) * 16 + zc, lax.rem(s + i % 4, 4))


def zc_numbers(zc):
    return [
        lax.rem(zc // 2 + i // 2, 8) * 2 + lax.rem(lax.rem(zc, 2) + i % 2, 2) for i in range(16)
    ]


def sender(src, dst, send_sem, recv_sem):
    x, zc, s = coords()
    me = (zc * 4 + x) * 4 + s
    numbers = zc_numbers(zc)

    def send(tile, sub):
        pltpu.make_async_remote_copy(
            src_ref=src.at[tile * 4 + sub],
            dst_ref=dst.at[me],
            send_sem=send_sem,
            recv_sem=recv_sem,
            device_id=(tile, sub),
            device_id_type=MESH,
        ).start()

    def near():
        for number in numbers[1:]:
            send(x * 16 + number, s)

        def one(i, carry):
            send(lax.rem(x + i // 4, 4) * 16 + zc, lax.rem(s + lax.rem(i, 4), 4))
            return carry

        lax.fori_loop(1, 16, one, 0)

    def far():
        def one(i, carry):
            first = lax.rem(x + i // 4, 4) * 16
            sub = lax.rem(s + lax.rem(i, 4), 4)
            for number in numbers[1:]:
                send(first + number, sub)
            return carry

        lax.fori_loop(1, 16, one, 0)

    return near, far


def send_group(peer, number, src, dst, me, send_sem, recv_sem):
    x, zc, s = coords()
    for i in range(1, 16):
        device = peer(i, x, zc, s)
        pltpu.make_async_remote_copy(
            src_ref=src.at[number(device)],
            dst_ref=dst.at[me],
            send_sem=send_sem,
            recv_sem=recv_sem,
            device_id=device,
            device_id_type=MESH,
        ).start()


def choose_cells(picks, choose):
    pick = picks[...].reshape(16, 64).astype(F32)
    pick = jnp.concatenate([pick, jnp.zeros((16, 64), F32)], axis=1).T[:64]
    pick = jnp.broadcast_to(pick.reshape(64, 1, 16), (64, 16, 16)).reshape(N_DEV * 4, 16)
    row = lax.broadcasted_iota(jnp.int32, (N_DEV * 4, 16), 0)
    lane = lax.broadcasted_iota(jnp.int32, (N_DEV * 4, 16), 1)
    column = jnp.sum(jnp.where(lane == lax.rem(row, 16), pick, 0.0), axis=1, keepdims=True)
    cell = lax.broadcasted_iota(jnp.int32, (N_DEV * 4, 512), 1)
    choose[...] = jnp.where(cell == column.astype(jnp.int32), 1.0, 0.0).astype(BF16)


OVER_CELLS = (((1,), (1,)), ((), ()))


def gather_rows(choose, spectra, first, size, dst):
    for lane in range(0, size, 256):
        width = min(256, size - lane)
        start = first + lane
        rows = lax.dot_general(
            choose[...], spectra[start : start + width, :], OVER_CELLS, preferred_element_type=F32
        )
        dst[:, :, lane : lane + width] = rows.astype(BF16).reshape(N_DEV, 4, width)


def gather_tail(choose, spectra, tail_send):
    last = lax.dot_general(
        choose[...], spectra[WIDE:, :], OVER_CELLS, preferred_element_type=F32
    )
    filler = jnp.zeros((64, NBIN - WIDE), F32)
    for zc in range(16):
        pieces = [last[(x * 16 + zc) * 16 : (x * 16 + zc) * 16 + 16] for x in range(4)]
        tail_send[zc] = jnp.concatenate(pieces + [filler], axis=0).T.astype(BF16)


def regroup_tail(tail_mid, tail_pass):
    turned = tail_mid[...].reshape(256, 128).T
    tail_pass[...] = turned[:64].reshape(16, 4, 256)


def finish_tail(tail_recv, table):
    turned = tail_recv[...].reshape(64, 256).T
    for zc in range(0, 16, 2):
        both = jnp.concatenate(
            [turned[zc * 16 : zc * 16 + 16], turned[zc * 16 + 16 : zc * 16 + 32]], axis=1
        )
        table[WIDE:, zc * 64 : zc * 64 + 128] = both


def pack_halo(floe, courant, row_send, col_send):
    for n in range(5):
        row_send[0, n * 16 : n * 16 + 16] = floe[n, :, 0:4, :]
        row_send[1, n * 16 : n * 16 + 16] = floe[n, :, 4:8, :]
    row_send[0, 80:82] = courant[:, 0:4, :]
    row_send[1, 80:82] = courant[:, 4:8, :]
    filler = jnp.zeros((COLUMN_ROWS - 656, 128), F32)
    for side, lanes in ((0, slice(0, 128)), (1, slice(384, 512))):
        strip = jnp.concatenate(
            [floe[:, :, :, lanes].reshape(640, 128), courant[:, :, lanes].reshape(16, 128), filler]
        )
        turned = strip.T
        col_send[side] = turned[0:8] if side == 0 else turned[120:128]


def halo_copies(row_send, row_recv, col_send, col_recv, send_sem, recv_sem):
    t, s = lax.axis_index("tiles"), lax.axis_index("sub")
    n_tiles = lax.axis_size("tiles")
    copies = []

    def add(src, dst, device):
        k = len(copies)
        copies.append(
            pltpu.make_async_remote_copy(
                src_ref=src,
                dst_ref=dst,
                send_sem=send_sem.at[k],
                recv_sem=recv_sem.at[k],
                device_id=device,
                device_id_type=MESH,
            )
        )

    for side, step in ((0, n_tiles - 1), (1, 1)):
        for group, shift in ((0, 0), (1, 3), (2, 1)):
            device = (lax.rem(t + step, n_tiles), lax.rem(s + shift, 4))
            add(col_send.at[side], col_recv.at[side, group], device)
    add(row_send.at[0], row_recv.at[0], (t, lax.rem(s + 3, 4)))
    add(row_send.at[1], row_recv.at[1], (t, lax.rem(s + 1, 4)))
    return copies


def unpack_columns(col_recv, side):
    for group in range(3):
        side[group] = jnp.concatenate(
            [col_recv[0, group], jnp.zeros((112, COLUMN_ROWS), F32), col_recv[1, group]], axis=0
        ).T


def transport(floe, courant, row_recv, side, out):
    s = lax.axis_index("sub")
    row = lax.broadcasted_iota(jnp.int32, (8, 128), 0)

    def frame(own, layer):
        start = layer * 8 if isinstance(layer, int) else pl.multiple_of(layer * 8, 8)
        here = pl.ds(start, 8)
        corner = jnp.where(row < 4, side[1, here], side[2, here])
        top = jnp.concatenate([own, side[0, here]], axis=1)
        halo = jnp.concatenate([row_recv[0, layer], row_recv[1, layer]], axis=0)
        return top, jnp.concatenate([halo, corner], axis=1)

    wide_row = lax.broadcasted_iota(jnp.int32, (8, 640), 0)
    after, before = jnp.where(s < 3, 1.0, 0.0), jnp.where(s > 0, 1.0, 0.0)
    inside = jnp.where(wide_row < 4, after, before)
    parts = []
    for k in range(2):
        top, halo = frame(courant[k], 80 + k)
        parts.append(jnp.concatenate([top, halo * inside], axis=0))
    east, west = jnp.maximum(parts[0], 0.0), jnp.maximum(-parts[0], 0.0)
    north, south = jnp.maximum(parts[1], 0.0), jnp.maximum(-parts[1], 0.0)
    keep = 1.0 - east - west - north - south

    def one(layer):
        n, k = layer // 16, lax.rem(layer, 16)
        v = jnp.concatenate(frame(floe[n, k], layer), axis=0)
        for _ in range(NSUB):
            v = (
                v * keep
                + pltpu.roll(v * east, 1, 1)
                + pltpu.roll(v * west, 639, 1)
                + pltpu.roll(v * north, 1, 0)
                + pltpu.roll(v * south, 15, 0)
            )
        out[n, k] = v[0:8, 0:512]

    def pair(i, carry):
        one(2 * i)
        one(2 * i + 1)
        return carry

    lax.fori_loop(0, 40, pair, 0)


def transpose_in(src, table, first, width):
    for lane in range(0, width, 128):
        size = min(128, width - lane)
        block = src[:, :, lane : lane + 128].reshape(N_DEV * 4, 128)
        turned = block.T
        table[first + lane : first + lane + size, :] = turned[:size]


def build_mixing(r, slot, weight, mixing):
    rows = lax.broadcasted_iota(jnp.int32, (N_DEV * 4, 512), 0).astype(jnp.int16)
    total = jnp.zeros((N_DEV * 4, 512), BF16)
    for k in range(4):
        given = slot[k, pl.ds(r, 1), :]
        slots = lax.rem(given // 16, 16) * 64 + given // 256 * 16 + lax.rem(given, 16)
        slots = slots.astype(jnp.int16)
        weights = weight[k, pl.ds(r, 1), :].astype(BF16)
        total = total + jnp.where(rows == slots, weights, jnp.zeros((), BF16))
    mixing[r] = total


def wide(column, lanes=4):
    return jnp.concatenate([column] * lanes, axis=1)


def fill_decay(decay, decay_table):
    row = lax.broadcasted_iota(jnp.int32, (72, 128), 0)
    for g in range(18):
        decay_table[g * 72 : g * 72 + 72, :] = jnp.where(row < 36, decay[2 * g], decay[2 * g + 1])


def fill_paths(thick, edge, paths):
    direction = lax.rem(lax.broadcasted_iota(jnp.int32, (72, 128), 0), NDIR).astype(F32)
    angle = 2.0 * math.pi * direction / NDIR - math.pi
    trig = (jnp.cos(angle), jnp.sin(angle))
    cos_edge, sin_edge = jnp.cos(edge[...]), jnp.sin(edge[...])
    scaled = -math.log2(math.e) * thick[...]
    for r in range(8):
        cosine = wide(trig[0]) * cos_edge[r : r + 1] + wide(trig[1]) * sin_edge[r : r + 1]
        paths[r] = scaled[r : r + 1] / (0.25 + 0.75 * cosine * cosine)


def damping(r, start, size, decay_table, paths):
    path = paths[r]
    first = start % 72
    pieces, have = [path[first:]], 72 - first
    while have < size:
        pieces.append(path)
        have += 72
    factor = jnp.concatenate(pieces, axis=0)[:size]
    return jnp.exp2(wide(decay_table[start : start + size, :]) * factor)


def attenuate(r, steps, table, mixing, damp, att):
    for start, size in steps:
        spectrum = jnp.dot(table[start : start + size, :], mixing[r], preferred_element_type=F32)
        att[start : start + size, :] = (spectrum * damp(r, start, size)).astype(BF16)


def fracture(hist, weight, ice, brk, out):
    total_w = weight[0] + weight[1] + weight[2] + weight[3]
    used_w = sum(weight[k].astype(BF16).astype(F32) for k in range(4))
    fix = total_w / used_w
    rows = [hist[j] * fix for j in range(16)]
    total = functools.reduce(jnp.add, rows)
    strength = ice[...].astype(F32) * total / (total + 0.005 * 16 * NBIN)
    scale = strength / total
    share = [v * scale for v in rows]
    shorter, run = [], jnp.zeros_like(total)
    for j in range(16):
        shorter.append(run)
        run = run + share[j]
    brk_rows = brk[...]
    for n in range(5):
        above = jnp.zeros_like(total)
        for k in range(15, -1, -1):
            value = out[n, k]
            breakable = jnp.where(brk_rows <= k, value, 0.0)
            out[n, k] = value - breakable * shorter[k] + above * share[k]
            above = above + breakable


STEPS = (
    ((0, 256), (256, 320), (576, 320)),
    ((896, 256),),
    ((1152, 144),),
)
UNROLL = (2, 2, 8)


def kernel(
    decay_hbm, floe_hbm, courant_hbm, spectra_hbm, picks_hbm, slot_hbm, weight_hbm, thick_hbm, edge_hbm,
    strain_hbm, ice_hbm, brk_hbm, out,
    decay, floe, courant, spectra, picks, slot, weight, thick, edge, strain, ice, brk,
    choose, x0, x1, x2, r0, r1, r2, tail_send, tail_mid, tail_pass, tail_recv,
    row_send, row_recv, col_send, col_recv, side,
    table, mixing, decay_table, paths, last_damping, att, hist,
    load_sem, send_sem, recv_sem, own_sem, halo_send, halo_recv, group_sem
):
    x, zc, s = coords()
    me = (x * 16 + zc) * 4 + s
    me_slot = (zc * 4 + x) * 4 + s
    barrier = pltpu.get_barrier_semaphore()
    for i in range(1, 16):
        pl.semaphore_signal(barrier, inc=1, device_id=zc_peer(i, x, zc, s), device_id_type=MESH)
        pl.semaphore_signal(barrier, inc=1, device_id=xy_peer(i, x, zc, s), device_id_type=MESH)
    pairs = (
        (picks_hbm, picks), (spectra_hbm, spectra), (floe_hbm, floe), (courant_hbm, courant),
        (slot_hbm, slot), (weight_hbm, weight), (thick_hbm, thick), (edge_hbm, edge),
        (strain_hbm, strain), (ice_hbm, ice), (brk_hbm, brk), (decay_hbm, decay),
    )
    loads = [
        pltpu.make_async_copy(src, dst, load_sem.at[k]) for k, (src, dst) in enumerate(pairs)
    ]
    for copy in loads:
        copy.start()
    loads[0].wait()
    choose_cells(picks, choose)
    pl.semaphore_wait(barrier, 30)
    for i in range(1, 16):
        pl.semaphore_signal(group_sem, inc=1, device_id=xy_peer(i, x, zc, s), device_id_type=MESH)
    loads[1].wait()
    sends, lands = (x0, x1, x2), (r0, r1, r2)
    senders = [
        sender(sends[k], lands[k], send_sem.at[k], recv_sem.at[k]) for k in range(3)
    ]
    gather_rows(choose, spectra, *RANGES[0], x0)
    senders[0][0]()
    gather_tail(choose, spectra, tail_send)
    for copy in loads[2:]:
        copy.wait()
    pack_halo(floe, courant, row_send, col_send)
    pl.semaphore_wait(group_sem, 15)

    def zc_number(device):
        return lax.rem(device[0], 16)

    def xy_number(device):
        return device[0] // 16 * 4 + device[1]

    halo = halo_copies(row_send, row_recv, col_send, col_recv, halo_send, halo_recv)
    for copy in halo:
        copy.start()
    own = [
        pltpu.make_async_copy(sends[k].at[me], lands[k].at[me_slot], own_sem.at[k])
        for k in range(3)
    ]
    own.append(pltpu.make_async_copy(tail_send.at[zc], tail_mid.at[zc], own_sem.at[3]))
    own[3].start()
    send_group(zc_peer, zc_number, tail_send, tail_mid, zc, send_sem.at[3], recv_sem.at[3])
    senders[0][1]()
    own[0].start()

    fifteen = pl.ds(0, 15)
    own[3].wait()
    pltpu.make_async_copy(tail_send.at[fifteen], tail_mid.at[fifteen], recv_sem.at[3]).wait()
    regroup_tail(tail_mid, tail_pass)
    own_tail = pltpu.make_async_copy(
        tail_pass.at[x * 4 + s], tail_recv.at[x * 4 + s], own_sem.at[4]
    )
    own_tail.start()
    send_group(xy_peer, xy_number, tail_pass, tail_recv, x * 4 + s, send_sem.at[4], recv_sem.at[4])
    for k in (1, 2):
        gather_rows(choose, spectra, *RANGES[k], sends[k])
        own[k].start()
    senders[1][0]()
    senders[1][1]()

    fill_decay(decay, decay_table)
    fill_paths(thick, edge, paths)

    def mix_row(r, carry):
        build_mixing(r, slot, weight, mixing)
        last_damping[r] = damping(r, *STEPS[2][0], decay_table, paths)
        return carry

    lax.fori_loop(0, 8, mix_row, 0)
    for copy in halo:
        copy.wait()
    unpack_columns(col_recv, side)
    transport(floe, courant, row_recv, side, out)

    senders[2][0]()
    senders[2][1]()
    def damp(r, start, size):
        if (start, size) == STEPS[2][0]:
            return last_damping[r]
        return damping(r, start, size, decay_table, paths)

    others = pl.ds(0, N_DEV - 1)
    for k, (first, size) in enumerate(RANGES):
        if k == 2:
            own_tail.wait()
            pltpu.make_async_copy(
                tail_pass.at[fifteen], tail_recv.at[fifteen], recv_sem.at[4]
            ).wait()
            finish_tail(tail_recv, table)
        own[k].wait()
        pltpu.make_async_copy(sends[k].at[others], lands[k].at[others], recv_sem.at[k]).wait()
        transpose_in(lands[k], table, first, size)
        bins = slice(STEPS[k][0][0], sum(STEPS[k][-1]))

        def some_rows(i, carry):
            for u in range(UNROLL[k]):
                r = i * UNROLL[k] + u
                attenuate(r, STEPS[k], table, mixing, damp, att.at[u])
                part = jnp.dot(strain[:, bins], att[u, bins], preferred_element_type=F32)
                here = pl.ds(r, 1)
                hist[:, here, :] = part[:, None] if k == 0 else hist[:, here, :] + part[:, None]
            return carry

        lax.fori_loop(0, 8 // UNROLL[k], some_rows, 0)
    fracture(hist, weight, ice, brk, out)
    for k in range(3):
        pltpu.make_async_copy(sends[k].at[others], lands[k].at[others], send_sem.at[k]).wait()
    pltpu.make_async_copy(tail_send.at[fifteen], tail_mid.at[fifteen], send_sem.at[3]).wait()
    pltpu.make_async_copy(tail_pass.at[fifteen], tail_recv.at[fifteen], send_sem.at[4]).wait()


def shards(
    floe_area, courant, spectra, send_rows, src_slot, src_weight, thickness, edge_angle,
    decay_rate, strain_table, ice_mask, break_bin
):
    operands = (
        floe_area, courant, spectra[0, 0].T, jnp.transpose(send_rows[0, 0], (1, 2, 0)), src_slot,
        src_weight, thickness, edge_angle, strain_table, ice_mask, break_bin
    )
    anywhere = pl.BlockSpec(memory_space=pl.ANY)
    return pl.pallas_call(
        kernel,
        out_shape=pltpu.VMEM(floe_area.shape, F32),
        in_specs=[anywhere] * (len(operands) + 1),
        out_specs=pl.BlockSpec(memory_space=pltpu.VMEM),
        scratch_shapes=[pltpu.SMEM(decay_rate.shape, F32)]
        + [pltpu.VMEM(v.shape, v.dtype) for v in operands]
        + [
            pltpu.VMEM((N_DEV * 4, 512), BF16),
            *[pltpu.VMEM((N_DEV, 4, size), BF16) for _, size in RANGES],
            *[pltpu.VMEM((N_DEV, 4, size), BF16) for _, size in RANGES],
            pltpu.VMEM((16, 16, 128), BF16),
            pltpu.VMEM((16, 16, 128), BF16),
            pltpu.VMEM((16, 4, 256), BF16),
            pltpu.VMEM((16, 4, 256), BF16),
            pltpu.VMEM((2, 82, 4, 512), F32),
            pltpu.VMEM((2, 82, 4, 512), F32),
            pltpu.VMEM((2, 8, COLUMN_ROWS), F32),
            pltpu.VMEM((2, 3, 8, COLUMN_ROWS), F32),
            pltpu.VMEM((3, COLUMN_ROWS, 128), F32),
            pltpu.VMEM((NBIN, N_DEV * 4), BF16),
            pltpu.VMEM((8, N_DEV * 4, 512), BF16),
            pltpu.VMEM((NBIN, 128), F32),
            pltpu.VMEM((8, 72, 512), F32),
            pltpu.VMEM((8, STEPS[2][0][1], 512), F32),
            pltpu.VMEM((8, NBIN, 512), BF16),
            pltpu.VMEM((16, 8, 512), F32),
            pltpu.SemaphoreType.DMA((len(operands) + 1,)),
            pltpu.SemaphoreType.DMA((5,)),
            pltpu.SemaphoreType.DMA((5,)),
            pltpu.SemaphoreType.DMA((5,)),
            pltpu.SemaphoreType.DMA((8,)),
            pltpu.SemaphoreType.DMA((8,)),
            pltpu.SemaphoreType.REGULAR,
        ],
        compiler_params=pltpu.CompilerParams(
            collective_id=0, has_side_effects=True, vmem_limit_bytes=56 << 20
        ),
    )(decay_rate, *operands)


def solution(mesh):
    in_specs = (
        P(None, None, "sub", "tiles"),
        P(None, "sub", "tiles"),
        P("tiles", "sub", None, None),
        P("tiles", "sub", None, None, None),
        P(None, "sub", "tiles"),
        P(None, "sub", "tiles"),
        P("sub", "tiles"),
        P("sub", "tiles"),
        P(),
        P(),
        P("sub", "tiles"),
        P("sub", "tiles"),
    )
    out_specs = P(None, None, "sub", "tiles")
    return jax.shard_map(shards, mesh=mesh, in_specs=in_specs, out_specs=out_specs, check_vma=False)
```
